256 devices in a mesh: section: 16 (over y, x_lo, core), tp: 16 (over x_hi, z).
Axes of the slice: x: 4 (x_hi: 2, x_lo: 2; x = x_hi * 2 + x_lo), y: 4, z: 8, core: 2. Of those that a mesh axis runs over, the one named last changes fastest.
Arguments:
- saved_queries: bfloat16 [16, 512, 7168], P('section', None, 'tp'), may hold values from -40 to 40
- saved_keys: bfloat16 [16, 512, 7168], P('section', None, 'tp'), may hold values from -40 to 40
- values: bfloat16 [16, 512, 7168], P('section', None, 'tp'), may hold values from -6 to 6
- attention_output_grad: bfloat16 [16, 512, 7168], P('section', None, 'tp'), may hold values from -0.59765625 to 0.59765625
- segments: int32 [512], replicated, may hold values from 0 to 5, never falling along the last dimension, each value on 1 to 256 neighbouring positions
- hidden: bfloat16 [16, 512, 3584], P('section'), may hold values from -6 to 6
- embedding: bfloat16 [512, 3584], replicated, may hold values from -6 to 6
- section_block_index: int32 [16, 1], replicated, may hold values from 0 to 1
- shared_query_weight: bfloat16 [2, 7168, 7168], P(None, 'section', 'tp'), may hold values from -0.0625 to 0.0625
- adapter_down_factor: bfloat16 [16, 7168, 128], P('section', 'tp'), may hold values from -0.0625 to 0.0625
- adapter_up_factor: bfloat16 [16, 128, 7168], P('section', None, 'tp'), may hold values from -0.5 to 0.5
- residual: bfloat16 [16, 512, 3584], P('section', 'tp'), may hold values from -0.59765625 to 0.59765625
Outputs:
- key_grad: bfloat16 [16, 512, 7168], P('section', None, 'tp')
- value_grad: bfloat16 [16, 512, 7168], P('section', None, 'tp')
- lora_down_grad: float32 [16, 7168, 128], P('section', 'tp')
- lora_up_grad: float32 [16, 128, 7168], P('section', None, 'tp')
- query_weight_grad: float32 [2, 7168, 7168], P(None, 'section', 'tp')
- passed_grad: bfloat16 [16, 512, 3584], P('section', 'tp')
- embed_grad: float32 [512, 3584], P('tp', 'section')
The draws below stay inside these ranges and needn't reach their ends.
All inputs are finite; a program needn't handle non-finite values.
Results may differ from the reference program's by a relative error of at most 0.017.
Values may be sent and summed in bfloat16 or wider, within the bound.
A program may use at most 128 MiB of HBM per device.

```python
import math
import jax
import jax.numpy as jnp
import numpy as np
from jax import lax

MODEL_WIDTH = 3584
HEADS = 32
ADAPTER_RANK = 128
WINDOW_TOKENS = 512
DOCS = 6
RELAY_SECTIONS = 16
LOCAL_QUERY_COLS = 448
N_TP = 16


def paired_base(key):
    full_shape = (RELAY_SECTIONS, WINDOW_TOKENS, 2 * MODEL_WIDTH)
    query_base = jnp.clip(jax.random.normal(jax.random.fold_in(key, 11), full_shape, jnp.float32), -5.0, 5.0)
    key_base = jnp.clip(jax.random.normal(jax.random.fold_in(key, 12), full_shape, jnp.float32), -5.0, 5.0)
    return (query_base, key_base)


def draw_saved_queries(key, part):
    query_base, key_base = paired_base(key)
    result = query_base
    return result.astype(jnp.bfloat16)


def draw_saved_keys(key, part):
    query_base, key_base = paired_base(key)
    result = key_base
    return result.astype(jnp.bfloat16)


def spiked(values, own_key, source, target, shards_of, factor):
    def block_of(position):
        return (jnp.arange(values.shape[position]) // (values.shape[position] // shards_of)).reshape((-1,) + (1,) * (values.ndim - 1 - position))

    first = jax.random.permutation(own_key, shards_of)[block_of(target)]
    far = (block_of(target) + shards_of // 2) % shards_of
    return jnp.where((block_of(source) == first) | (block_of(source) == far), factor * values, values)


def steps_of(own_key, dims, cuts, least, high):
    def one(position, blocks):
        draws = jax.random.uniform(jax.random.fold_in(jax.random.fold_in(own_key, 6), position), (blocks,), jnp.float32, least / len(cuts), high / len(cuts))
        return jnp.repeat(jnp.exp(draws), dims[position] // blocks).reshape((-1,) + (1,) * (len(dims) - position - 1))

    gain = one(*cuts[0])
    for cut in cuts[1:]:
        gain = gain * one(*cut)
    return gain


def different_ones(key, rows, number_of, top, lift):
    sequence = jax.random.permutation(jax.random.fold_in(key, 1), number_of)
    boost = sequence
    for power in range(3):
        boost = boost * boost // number_of
    boost = boost * lift // number_of
    chance = jax.random.randint(jax.random.fold_in(key, 2), (rows, number_of), 0, 4096) + boost
    holders = jax.random.permutation(jax.random.fold_in(key, 3), rows)[jnp.arange(number_of) % rows]
    chance = jnp.where(jnp.arange(rows)[:, None] == holders[None, :], 1 << 14, chance)
    score = chance * number_of + jnp.arange(number_of)
    return lax.top_k(score.astype(jnp.int32), top)[1].astype(jnp.int32)


def length_profile(number_of, total, most, slope):
    weights = [(1 << 20) // math.isqrt(grade ** slope) + 1 for grade in range(2, number_of + 1)]
    rest, given = total - most - (number_of - 1), [1] * (number_of - 1)
    while rest > 0:
        movable = [i for i in range(number_of - 1) if given[i] < most]
        whole, left = sum([weights[i] for i in movable]), rest
        for i in movable:
            more = min(most - given[i], max(1, left * weights[i] // whole), rest)
            given[i] = given[i] + more
            rest = rest - more
    return np.array([most] + given)


def uneven(own_key, count, total, limit, lean):
    if count == 2:
        one = jax.random.randint(own_key, (), max(1, total - limit), min(limit, total - 1) + 1)
        return jnp.stack([one, total - one])
    sizes = jnp.asarray(length_profile(count, total, limit, lean), jnp.int32)
    couples = (count - 1) // 2
    giver, taker = sizes[1:1 + 2 * couples:2], sizes[2:2 + 2 * couples:2]
    margin = jnp.minimum(giver - 1, limit - taker)
    passed = jax.random.randint(jax.random.fold_in(own_key, 1), (couples,), 0, 1 << 20) % (margin + 1)
    sizes = sizes.at[1:1 + 2 * couples:2].set(giver - passed).at[2:2 + 2 * couples:2].set(taker + passed)
    return sizes[jax.random.permutation(jax.random.fold_in(own_key, 2), count)]


def bell_draw(own_key, extent, spread, reach, shards=(), kind=jnp.bfloat16):
    gain = steps_of(own_key, extent, shards, -0.22, 0.18) if shards else 1.0
    values = jax.random.normal(own_key, extent, jnp.float32) * spread * gain
    return jnp.minimum(jnp.maximum(values, -reach), reach).astype(kind)


def heavy_noise(rng, shape, scale, bound, pieces, heavy, kind=jnp.bfloat16):
    values = scale * jax.random.normal(rng, shape, jnp.float32)
    if pieces:
        values = values * steps_of(rng, shape, pieces, -0.22, 0.18)
    return jnp.clip(spiked(values, jax.random.fold_in(rng, 3), *heavy), -bound, bound).astype(kind)


def setup_inputs(seed: int = 0) -> dict:
    arg_keys = jax.random.split(jax.random.key(seed), 13)
    return {
        "saved_queries": draw_saved_queries(jax.random.fold_in(arg_keys[12], 71), 0),
        "saved_keys": draw_saved_keys(jax.random.fold_in(arg_keys[12], 71), 0),
        "values": bell_draw(arg_keys[2], (RELAY_SECTIONS, WINDOW_TOKENS, 2 * MODEL_WIDTH), 1.0, 6.0, ((0, 16), (2, 16))),
        "attention_output_grad": bell_draw(arg_keys[3], (RELAY_SECTIONS, WINDOW_TOKENS, 2 * MODEL_WIDTH), 0.1, 0.59765625, ((0, 16), (2, 16))),
        "segments": jnp.searchsorted(jnp.cumsum(uneven(arg_keys[4], DOCS, WINDOW_TOKENS, WINDOW_TOKENS // 2, 0)), jnp.arange(WINDOW_TOKENS), side="right").astype(jnp.int32),
        "hidden": heavy_noise(arg_keys[5], (RELAY_SECTIONS, WINDOW_TOKENS, MODEL_WIDTH), 1.0, 6.0, ((0, 16),), (0, 2, 16, 2.0)),
        "embedding": bell_draw(arg_keys[6], (WINDOW_TOKENS, MODEL_WIDTH), 1.0, 6.0),
        "section_block_index": different_ones(arg_keys[7], RELAY_SECTIONS, 2, 1, 0),
        "shared_query_weight": bell_draw(arg_keys[8], (2, 2 * MODEL_WIDTH, 2 * MODEL_WIDTH), (2 * MODEL_WIDTH) ** -0.5, 0.0625, ((1, 16), (2, 16))),
        "adapter_down_factor": bell_draw(arg_keys[9], (RELAY_SECTIONS, 2 * MODEL_WIDTH, ADAPTER_RANK), (2 * MODEL_WIDTH) ** -0.5, 0.0625, ((0, 16), (1, 16))),
        "adapter_up_factor": bell_draw(arg_keys[10], (RELAY_SECTIONS, ADAPTER_RANK, 2 * MODEL_WIDTH), ADAPTER_RANK ** -0.5, 0.5, ((0, 16), (2, 16))),
        "residual": bell_draw(arg_keys[11], (RELAY_SECTIONS, WINDOW_TOKENS, MODEL_WIDTH), 0.1, 0.59765625, ((0, 16), (1, 16))),
    }


def settle(array):
    return lax.optimization_barrier(array.astype(jnp.bfloat16)).astype(jnp.float32)


def attention_grads(saved_queries, saved_keys, values, attention_output_grad, segments, head_count):
    tokens = saved_queries.shape[0]
    head_width = saved_queries.shape[1] // head_count
    score_scale = head_width ** -0.5
    head_shape = (tokens, head_count, head_width)
    query_heads = saved_queries.astype(jnp.float32).reshape(head_shape)
    key_heads = saved_keys.astype(jnp.float32).reshape(head_shape)
    value_heads = values.astype(jnp.float32).reshape(head_shape)
    grad_heads = attention_output_grad.astype(jnp.float32).reshape(head_shape)
    scores = jnp.einsum("thd,shd->hts", query_heads, key_heads, precision=lax.Precision.HIGHEST) * score_scale
    positions = jnp.arange(tokens)
    allowed = (positions[:, None] >= positions[None, :]) & (segments[:, None] == segments[None, :])
    scores = jnp.where(allowed[None], scores, -1.0e30)
    row_top = jnp.max(scores, axis=2, keepdims=True)
    expsum = jnp.exp(scores - row_top)
    soft_weights = expsum / jnp.sum(expsum, axis=2, keepdims=True)
    probs_low = settle(soft_weights)
    attended = jnp.einsum("hts,shd->thd", probs_low, value_heads, precision=lax.Precision.HIGHEST)
    row_delta = jnp.sum(grad_heads * attended, axis=2)
    prob_grad = jnp.einsum("thd,shd->hts", grad_heads, value_heads, precision=lax.Precision.HIGHEST)
    score_low = settle(soft_weights * (prob_grad - row_delta.T[:, :, None]))
    query_gradient = jnp.einsum("hts,shd->thd", score_low, key_heads, precision=lax.Precision.HIGHEST) * score_scale
    key_grad = jnp.einsum("hts,thd->shd", score_low, query_heads, precision=lax.Precision.HIGHEST) * score_scale
    value_grad = jnp.einsum("hts,thd->shd", probs_low, grad_heads, precision=lax.Precision.HIGHEST)
    return (query_gradient.reshape(tokens, -1).astype(jnp.bfloat16), key_grad.reshape(tokens, -1).astype(jnp.bfloat16),
            value_grad.reshape(tokens, -1).astype(jnp.bfloat16))


def reference(saved_queries, saved_keys, values, attention_output_grad, segments, hidden, embedding, section_block_index, shared_query_weight, adapter_down_factor, adapter_up_factor, residual):
    weight_grad = jnp.zeros((2, 2 * MODEL_WIDTH, 2 * MODEL_WIDTH), jnp.float32)
    embed_grad = jnp.zeros((WINDOW_TOKENS, MODEL_WIDTH), jnp.float32)
    identity_tensor_split = jnp.eye(N_TP, dtype=jnp.float32)
    key_list, value_list, down_list, up_list, sent_list = [], [], [], [], []
    for section_adapter_rank in range(RELAY_SECTIONS):
        joined_pieces = jnp.concatenate([hidden[section_adapter_rank], embedding], axis=1)
        query_gradient, key_grad, value_grad = attention_grads(saved_queries[section_adapter_rank], saved_keys[section_adapter_rank], values[section_adapter_rank],
                                                           attention_output_grad[section_adapter_rank], segments, HEADS)
        key_list.append(key_grad)
        value_list.append(value_grad)
        block_index = section_block_index[section_adapter_rank, 0]
        weight_term = settle(jnp.dot(joined_pieces.T, query_gradient, preferred_element_type=jnp.float32))
        weight_grad = weight_grad.at[block_index].add(weight_term)
        reduced_rank_term = jnp.dot(joined_pieces, adapter_down_factor[section_adapter_rank], preferred_element_type=jnp.float32).astype(jnp.bfloat16)
        returned_rank = jnp.dot(query_gradient, adapter_up_factor[section_adapter_rank].T, preferred_element_type=jnp.float32).astype(jnp.bfloat16)
        up_list.append(jnp.dot(reduced_rank_term.T, query_gradient, preferred_element_type=jnp.float32))
        down_list.append(jnp.dot(joined_pieces.T, returned_rank, preferred_element_type=jnp.float32))
        chosen_weight = shared_query_weight[block_index]
        grad_split = query_gradient.astype(jnp.float32).reshape(WINDOW_TOKENS, N_TP, LOCAL_QUERY_COLS)
        weight_split = chosen_weight.astype(jnp.float32).reshape(2 * MODEL_WIDTH, N_TP, LOCAL_QUERY_COLS)
        tensor_split_parts = jnp.einsum("tnh,fnh->ntf", grad_split, weight_split, precision=lax.Precision.HIGHEST)
        adapter_columns = jnp.dot(returned_rank, adapter_down_factor[section_adapter_rank].T, preferred_element_type=jnp.float32).reshape(WINDOW_TOKENS, N_TP, LOCAL_QUERY_COLS)
        tensor_split_parts = tensor_split_parts.reshape(N_TP, WINDOW_TOKENS, N_TP, LOCAL_QUERY_COLS) + identity_tensor_split[:, None, :, None] * adapter_columns[None]
        summed = jnp.sum(settle(tensor_split_parts), axis=0).reshape(WINDOW_TOKENS, 2 * MODEL_WIDTH)
        sent_list.append((residual[section_adapter_rank].astype(jnp.float32) + summed[:, :MODEL_WIDTH]).astype(jnp.bfloat16))
        embed_grad = embed_grad + summed[:, MODEL_WIDTH:]
    passed_grad = jnp.stack(sent_list[1:] + [jnp.zeros((WINDOW_TOKENS, MODEL_WIDTH), jnp.bfloat16)])
    return (jnp.stack(key_list), jnp.stack(value_list), jnp.stack(down_list), jnp.stack(up_list), weight_grad,
            passed_grad, embed_grad)
```

```python
import functools

import jax
import jax.numpy as jnp
from jax import lax
from jax.experimental import pallas as pl
from jax.experimental.pallas import tpu as pltpu
from jax.sharding import PartitionSpec as P

MESH = pl.DeviceIdType.MESH
TOKENS = 512
WIDTH = 3584
COLS = 448
HD = 224
RANK = 128
WIN = 512
NSEC = 16
NTP = 16
SPLIT = 128
VMEM_LIMIT = 60 * 1024 * 1024
F32 = jnp.float32
BF16 = jnp.bfloat16


def dot_nt(a, b):
    return lax.dot_general(a, b, (((1,), (1,)), ((), ())), preferred_element_type=F32)


def dot_tn(a, b):
    return lax.dot_general(a, b, (((0,), (0,)), ((), ())), preferred_element_type=F32)


def dot_nn(a, b):
    return lax.dot_general(a, b, (((1,), (0,)), ((), ())), preferred_element_type=F32)


def remote(src, dst, send_sem, recv_sem, section, tp):
    return pltpu.make_async_remote_copy(
        src_ref=src,
        dst_ref=dst,
        send_sem=send_sem,
        recv_sem=recv_sem,
        device_id={"section": section, "tp": tp},
        device_id_type=MESH,
    )


def greet(peers):
    barrier = pltpu.get_barrier_semaphore()
    for section, tp in peers:
        pl.semaphore_signal(
            barrier, inc=1, device_id={"section": section, "tp": tp}, device_id_type=MESH
        )
    pl.semaphore_wait(barrier, len(peers))


def attention(q_ref, k_ref, v_ref, g_ref, segc_ref, segr_ref, qg, kacc, vacc):
    scale = HD ** (-0.5)
    lane = lax.broadcasted_iota(jnp.int32, (1, COLS), 1)
    kacc[...] = jnp.zeros_like(kacc)
    vacc[...] = jnp.zeros_like(vacc)
    rows = 256
    for block in range(TOKENS // rows):
        top = block * rows
        cols = top + rows
        here = pl.ds(top, rows)
        upto = pl.ds(0, cols)
        row_id = lax.broadcasted_iota(jnp.int32, (rows, cols), 0) + top
        col_id = lax.broadcasted_iota(jnp.int32, (rows, cols), 1)
        allowed = (row_id >= col_id) & (segc_ref[here, :] == segr_ref[:, upto])
        dq = None
        for head in range(2):
            mask = jnp.where((lane >= HD) == (head == 1), 1.0, 0.0).astype(BF16)
            q = q_ref[here, :] * mask
            g = g_ref[here, :] * mask
            k = k_ref[upto, :]
            scores = dot_nt(q, k) * scale
            scores = jnp.where(allowed, scores, -1e30)
            top_score = jnp.max(scores, axis=1, keepdims=True)
            expo = jnp.exp(scores - top_score)
            probs = expo / jnp.sum(expo, axis=1, keepdims=True)
            low = probs.astype(BF16)
            grad = dot_nt(g, v_ref[upto, :])
            delta = jnp.sum(low.astype(F32) * grad, axis=1, keepdims=True)
            dscore = (probs * (grad - delta)).astype(BF16)
            part = dot_nn(dscore, k * mask)
            dq = part if dq is None else dq + part
            kacc[upto, :] += dot_tn(dscore, q)
            vacc[upto, :] += dot_tn(low, g)
        qg[here, :] = (dq * scale).astype(BF16)


def first_kernel(
    q_ref, k_ref, v_ref, g_ref, segc_ref, segr_ref, up_ref, hidden, weight,
    kg_ref, vg_ref, back_ref, qg4, hid4, wg,
    qg, kacc, vacc, bpart, bland, bown, ball,
    loc_sem, hs_sem, hr_sem, ws_sem, wr_sem, qs_sem, qr_sem, bs_sem, br_sem, cs_sem, cr_sem,
):
    s = lax.axis_index("section")
    t = lax.axis_index("tp")
    y, j = s // 4, s % 4
    lo, c = j // 2, j % 2
    hi, z = t // 8, t % 8
    sib = y * 4 + 2 * lo + (1 - c)
    across = [y * 4 + 2 * (1 - lo) + i for i in range(2)]
    t_far = (1 - hi) * 8 + z
    left = ((y + 3) % 4) * 4 + j
    right = ((y + 1) % 4) * 4 + j
    tp_peers = [(t + i) % NTP for i in range(1, NTP)]
    greet(
        [(sib, t), (left, t), (right, t)]
        + [(a, t) for a in across]
        + [(a, t_far) for a in across]
        + [(s, p) for p in tp_peers]
    )

    def row_block(b, owner_y):
        return wg.at[b, pl.ds(pl.multiple_of(owner_y * COLS, 64), COLS), :]

    wsends = []
    for n, (b, dest, slot) in enumerate([(0, right, 0), (1, left, 3), (1, right, 1), (0, left, 2)]):
        copy = remote(weight.at[b], row_block(b, y), ws_sem.at[n], wr_sem.at[slot], dest, t)
        copy.start()
        wsends.append(copy)

    def window(lo_d, c_d, part):
        start = pl.multiple_of(896 * lo_d + 384 * c_d + 1792 * part, 128)
        return pl.ds(start, WIN)

    hsends = []
    for part in range(2):
        for i in range(2):
            near = remote(
                hidden.at[pl.ds(0, SPLIT), window(1 - lo, i, part)],
                hid4.at[j, part, pl.ds(0, SPLIT), :],
                hs_sem.at[len(hsends)], hr_sem.at[2 + 2 * c + part], across[i], t,
            )
            near.start()
            hsends.append(near)
            far = remote(
                hidden.at[pl.ds(SPLIT, TOKENS - SPLIT), window(1 - lo, i, part)],
                hid4.at[j, part, pl.ds(SPLIT, TOKENS - SPLIT), :],
                hs_sem.at[len(hsends)], hr_sem.at[6 + 2 * c + part], across[i], t_far,
            )
            far.start()
            hsends.append(far)
        twin = remote(
            hidden.at[:, window(lo, 1 - c, part)], hid4.at[j, part],
            hs_sem.at[len(hsends)], hr_sem.at[part], sib, t,
        )
        twin.start()
        hsends.append(twin)
    locals_ = []
    for part in range(2):
        copy = pltpu.make_async_copy(
            hidden.at[:, window(lo, c, part)], hid4.at[j, part], loc_sem.at[part]
        )
        copy.start()
        locals_.append(copy)
    for b in range(2):
        copy = pltpu.make_async_copy(weight.at[b], row_block(b, y), loc_sem.at[2 + b])
        copy.start()
        locals_.append(copy)

    attention(q_ref, k_ref, v_ref, g_ref, segc_ref, segr_ref, qg, kacc, vacc)

    qsends = []
    for n, dest in enumerate([across[0], across[1], sib]):
        copy = remote(qg, qg4.at[j], qs_sem.at[n], qr_sem.at[j], dest, t)
        copy.start()
        qsends.append(copy)
    copy = pltpu.make_async_copy(qg, qg4.at[j], loc_sem.at[4])
    copy.start()
    locals_.append(copy)

    yl, yr = (y + 3) % 4, (y + 1) % 4
    yo = (y + 2) % 4

    def wait_w(b, owner_y, slot):
        remote(weight.at[b], row_block(b, owner_y), ws_sem.at[0], wr_sem.at[slot], left, t).wait_recv()

    wait_w(0, yl, 0)
    copy = remote(row_block(0, yl), row_block(0, yl), ws_sem.at[4], wr_sem.at[4], right, t)
    copy.start()
    wsends.append(copy)
    wait_w(1, yr, 3)
    copy = remote(row_block(1, yr), row_block(1, yr), ws_sem.at[5], wr_sem.at[5], left, t)
    copy.start()
    wsends.append(copy)

    bpart[...] = dot_nt(qg[...], up_ref[...]).reshape(NTP, 32, RANK)
    bsends = []
    for n, peer in enumerate(tp_peers):
        copy = remote(bpart.at[peer], bland.at[t], bs_sem.at[n], br_sem.at[t], s, peer)
        copy.start()
        bsends.append(copy)
    kg_ref[...] = (kacc[...] * HD ** (-0.5)).astype(BF16)
    vg_ref[...] = vacc[...].astype(BF16)
    bland[t] = bpart[t]
    for peer in tp_peers:
        remote(bpart.at[peer], bland.at[peer], bs_sem.at[0], br_sem.at[peer], s, peer).wait_recv()
    bown[...] = jnp.sum(bland[...], axis=0).astype(BF16)
    csends = []
    for n, peer in enumerate(tp_peers):
        copy = remote(bown, ball.at[t], cs_sem.at[n], cr_sem.at[t], s, peer)
        copy.start()
        csends.append(copy)
    ball[t] = bown[...]
    for peer in tp_peers:
        remote(bown, ball.at[peer], cs_sem.at[0], cr_sem.at[peer], s, peer).wait_recv()
    back_ref[...] = ball[...]

    for slot in [sib % 4, across[0] % 4, across[1] % 4]:
        remote(qg, qg4.at[slot], qs_sem.at[0], qr_sem.at[slot], sib, t).wait_recv()
    wait_w(1, yl, 1)
    wait_w(0, yr, 2)
    wait_w(0, yo, 4)
    wait_w(1, yo, 5)
    for part in range(2):
        remote(
            hidden.at[:, window(lo, c, part)], hid4.at[j + 1 - 2 * c, part],
            hs_sem.at[0], hr_sem.at[part], sib, t,
        ).wait_recv()
        for i in range(2):
            slot = 2 * (1 - lo) + i
            for first, count, base in ((0, SPLIT, 2), (SPLIT, TOKENS - SPLIT, 6)):
                remote(
                    hidden.at[pl.ds(first, count), window(lo, c, part)],
                    hid4.at[slot, part, pl.ds(first, count), :],
                    hs_sem.at[0], hr_sem.at[base + 2 * i + part], sib, t,
                ).wait_recv()
    for copy in locals_:
        copy.wait()
    for copy in wsends + hsends + qsends + bsends + csends:
        copy.wait_send()


def first_call(q, k, v, g, segc, segr, up, hidden, weight):
    vm = pl.BlockSpec(memory_space=pltpu.VMEM)
    anys = pl.BlockSpec(memory_space=pl.ANY)
    dma = pltpu.SemaphoreType.DMA
    return pl.pallas_call(
        first_kernel,
        out_shape=(
            jax.ShapeDtypeStruct((TOKENS, COLS), BF16),
            jax.ShapeDtypeStruct((TOKENS, COLS), BF16),
            jax.ShapeDtypeStruct((NTP, 32, RANK), BF16),
            jax.ShapeDtypeStruct((4, TOKENS, COLS), BF16),
            jax.ShapeDtypeStruct((4, 2, TOKENS, WIN), BF16),
            jax.ShapeDtypeStruct((2, 4 * COLS, COLS), BF16),
        ),
        in_specs=[vm] * 7 + [anys] * 2,
        out_specs=(vm, vm, vm, anys, anys, anys),
        scratch_shapes=[
            pltpu.VMEM((TOKENS, COLS), BF16),
            pltpu.VMEM((TOKENS, COLS), F32),
            pltpu.VMEM((TOKENS, COLS), F32),
            pltpu.VMEM((NTP, 32, RANK), F32),
            pltpu.VMEM((NTP, 32, RANK), F32),
            pltpu.VMEM((32, RANK), BF16),
            pltpu.VMEM((NTP, 32, RANK), BF16),
            dma((5,)), dma((10,)), dma((10,)), dma((6,)), dma((6,)), dma((3,)), dma((4,)),
            dma((15,)), dma((16,)), dma((15,)), dma((16,)),
        ],
        compiler_params=pltpu.CompilerParams(
            collective_id=0, has_side_effects=True, vmem_limit_bytes=VMEM_LIMIT
        ),
        name="attention_and_exchange",
    )(q, k, v, g, segc, segr, up, hidden, weight)


def input_grad_kernel(ids, qg4_ref, wh_ref, we_ref, out_ref, qsum):
    i = pl.program_id(0)

    @pl.when(i == 0)
    def _():
        qsum[...] = jnp.zeros_like(qsum)

    @pl.when(i < 4)
    def _():
        out = dot_nt(qg4_ref[0], wh_ref[0])
        out_ref[...] = out.reshape(NTP, 1, 32, 2 * COLS).astype(BF16)
        qsum[ids[i]] += qg4_ref[0].astype(F32)

    @pl.when(i == 4)
    def _():
        out = dot_nt(qsum[0].astype(BF16), we_ref[0]) + dot_nt(qsum[1].astype(BF16), we_ref[1])
        out_ref[...] = out.reshape(NTP, 1, 32, 2 * COLS).astype(BF16)


def input_grad_call(ids, qg4, wg):
    return pl.pallas_call(
        input_grad_kernel,
        grid_spec=pltpu.PrefetchScalarGridSpec(
            num_scalar_prefetch=1,
            grid=(5,),
            in_specs=[
                pl.BlockSpec((1, TOKENS, COLS), lambda i, ids: (jnp.minimum(i, 3), 0, 0)),
                pl.BlockSpec((1, 2 * COLS, COLS), lambda i, ids: (ids[jnp.minimum(i, 3)], 0, 0)),
                pl.BlockSpec((2, 2 * COLS, COLS), lambda i, ids: (0, 1, 0)),
            ],
            out_specs=pl.BlockSpec((NTP, 1, 32, 2 * COLS), lambda i, ids: (0, i, 0, 0)),
            scratch_shapes=[pltpu.VMEM((2, TOKENS, COLS), F32)],
        ),
        out_shape=jax.ShapeDtypeStruct((NTP, 5, 32, 2 * COLS), BF16),
        compiler_params=pltpu.CompilerParams(vmem_limit_bytes=VMEM_LIMIT),
        cost_estimate=pl.CostEstimate(
            flops=2 * 6 * TOKENS * COLS * 2 * COLS, bytes_accessed=12 * 2**20, transcendentals=0
        ),
        name="input_grad",
    )(ids, qg4, wg, wg)


def weight_grad_kernel(ids, qg4_ref, hid_ref, emb_ref, out_ref, acc, qsum):
    i = pl.program_id(0)
    first = pl.multiple_of(64 * ids[4], 64)

    @pl.when(i == 0)
    def _():
        qsum[...] = jnp.zeros_like(qsum)
        for n in range(4):
            qsum[ids[n]] += qg4_ref[n].astype(F32)

    @pl.when(i < 2)
    def _():
        acc[...] = jnp.zeros_like(acc)
        for n in range(4):
            acc[ids[n]] += dot_tn(hid_ref[n, 0], qg4_ref[n])

    @pl.when(i >= 2)
    def _():
        for b in range(2):
            acc[b] = dot_tn(emb_ref[0], qsum[b].astype(BF16))

    for b in range(2):
        out_ref[0, b] = acc[b, pl.ds(first, COLS), :].astype(BF16)


def weight_grad_call(ids, qg4, hid4, emb):
    return pl.pallas_call(
        weight_grad_kernel,
        grid_spec=pltpu.PrefetchScalarGridSpec(
            num_scalar_prefetch=1,
            grid=(4,),
            in_specs=[
                pl.BlockSpec((4, TOKENS, COLS), lambda i, ids: (0, 0, 0)),
                pl.BlockSpec((4, 1, TOKENS, WIN), lambda i, ids: (0, jnp.minimum(i, 1), 0, 0)),
                pl.BlockSpec((1, TOKENS, WIN), lambda i, ids: (jnp.maximum(i - 2, 0), 0, 0)),
            ],
            out_specs=pl.BlockSpec((1, 2, COLS, COLS), lambda i, ids: (i, 0, 0, 0)),
            scratch_shapes=[pltpu.VMEM((2, WIN, COLS), F32), pltpu.VMEM((2, TOKENS, COLS), F32)],
        ),
        out_shape=jax.ShapeDtypeStruct((4, 2, COLS, COLS), BF16),
        compiler_params=pltpu.CompilerParams(vmem_limit_bytes=VMEM_LIMIT),
        cost_estimate=pl.CostEstimate(
            flops=2 * 12 * TOKENS * WIN * COLS, bytes_accessed=12 * 2**20, transcendentals=0
        ),
        name="weight_grad",
    )(ids, qg4, hid4, emb)


def second_kernel(
    dw, ae, base, wsum_ref, aesum_ref, next_base,
    dwl, ael, loc_sem, ws_sem, wr_sem, as_sem, ar_sem, b_sem,
):
    s = lax.axis_index("section")
    t = lax.axis_index("tp")
    y, j = s // 4, s % 4
    peers = [(s + i) % NSEC for i in range(1, NSEC)]
    greet([(p, t) for p in peers])
    sends = []
    for n, i in enumerate((1, 3, 2)):
        yd = (y + i) % 4
        copy = remote(dw.at[yd], dwl.at[y], ws_sem.at[n], wr_sem.at[y], yd * 4 + j, t)
        copy.start()
        sends.append(copy)
    own = pltpu.make_async_copy(dw.at[y], dwl.at[y], loc_sem)
    own.start()
    copy = remote(base, next_base, b_sem.at[0], b_sem.at[1], (s + NSEC - 1) % NSEC, t)
    copy.start()
    sends.append(copy)
    for n, p in enumerate(peers):
        send = remote(ae.at[p], ael.at[s], as_sem.at[n], ar_sem.at[s], p, t)
        send.start()
        sends.append(send)
    ael[s] = ae[s]
    for p in peers:
        remote(ae.at[p], ael.at[p], as_sem.at[0], ar_sem.at[p], p, t).wait_recv()
    aesum_ref[...] = jnp.sum(ael[...], axis=0)
    copy.wait_recv()
    own.wait()
    for i in (1, 3, 2):
        ys = (y + i) % 4
        remote(dw.at[ys], dwl.at[ys], ws_sem.at[0], wr_sem.at[ys], s, t).wait_recv()
    for b in range(2):
        total = dwl[0, b].astype(F32)
        for n in range(1, 4):
            total = total + dwl[n, b].astype(F32)
        wsum_ref[b] = total
    for send in sends:
        send.wait_send()


def second_call(dw, ae, base):
    vm = pl.BlockSpec(memory_space=pltpu.VMEM)
    anys = pl.BlockSpec(memory_space=pl.ANY)
    dma = pltpu.SemaphoreType.DMA
    return pl.pallas_call(
        second_kernel,
        out_shape=(
            jax.ShapeDtypeStruct((2, COLS, COLS), F32),
            jax.ShapeDtypeStruct((32, HD), F32),
            jax.ShapeDtypeStruct((32, WIDTH), F32),
        ),
        in_specs=[anys, vm, anys],
        out_specs=(vm, vm, anys),
        scratch_shapes=[
            pltpu.VMEM((4, 2, COLS, COLS), BF16),
            pltpu.VMEM((NSEC, 32, HD), F32),
            dma, dma((3,)), dma((4,)), dma((15,)), dma((16,)), dma((2,)),
        ],
        compiler_params=pltpu.CompilerParams(
            collective_id=1, has_side_effects=True, vmem_limit_bytes=VMEM_LIMIT
        ),
        cost_estimate=pl.CostEstimate(flops=10**9, bytes_accessed=100 * 2**20, transcendentals=0),
        name="weight_sum",
    )(dw, ae, base)


def third_kernel(red, emb, pland, eland, ps_sem, pr_sem, es_sem, er_sem, loc_sem):
    s = lax.axis_index("section")
    t = lax.axis_index("tp")
    y, j = s // 4, s % 4
    peers = [(s + i) % NSEC for i in range(1, NSEC)]
    greet([(p, t) for p in peers])

    def move(src, dst, send_sem, recv_sem, here_sem, dest):
        away = remote(src, dst, send_sem, recv_sem, dest, t)
        here = pltpu.make_async_copy(src, dst, here_sem)

        @pl.when(dest != s)
        def _():
            away.start()

        @pl.when(dest == s)
        def _():
            here.start()

        def finish():
            @pl.when(dest != s)
            def _():
                away.wait_send()

            @pl.when(dest == s)
            def _():
                here.wait()

        return finish

    ends = []
    for n in range(4):
        dest = (y * 4 + n + NSEC - 1) % NSEC
        ends.append(move(red.at[n], pland.at[j], ps_sem.at[n], pr_sem.at[j], loc_sem.at[n], dest))
    for n in range(4):
        dest = 2 * j + n % 2 + 8 * (n // 2)
        ends.append(move(emb.at[n], eland.at[y], es_sem.at[n], er_sem.at[y], loc_sem.at[4 + n], dest))
    for n in range(4):
        source = (((s + 1) % NSEC) // 4) * 4 + n

        @pl.when(source != s)
        def _():
            remote(red.at[n], pland.at[n], ps_sem.at[n], pr_sem.at[n], source, t).wait_recv()

    for n in range(4):
        source = n * 4 + (s % 8) // 2

        @pl.when(source != s)
        def _():
            remote(emb.at[n], eland.at[n], es_sem.at[n], er_sem.at[n], source, t).wait_recv()

    for end in ends:
        end()


def third_call(red, emb):
    anys = pl.BlockSpec(memory_space=pl.ANY)
    dma = pltpu.SemaphoreType.DMA
    return pl.pallas_call(
        third_kernel,
        out_shape=(
            jax.ShapeDtypeStruct((4, 32, 2 * COLS), BF16),
            jax.ShapeDtypeStruct((4, 32, HD), BF16),
        ),
        in_specs=[anys, anys],
        out_specs=(anys, anys),
        scratch_shapes=[dma((4,)), dma((4,)), dma((4,)), dma((4,)), dma((8,))],
        compiler_params=pltpu.CompilerParams(
            collective_id=2, has_side_effects=True, vmem_limit_bytes=VMEM_LIMIT
        ),
        name="final_exchange",
    )(red, emb)


def on_device(
    saved_queries,
    saved_keys,
    values,
    attention_output_grad,
    segments,
    hidden,
    embedding,
    section_block_index,
    shared_query_weight,
    adapter_down_factor,
    adapter_up_factor,
    residual,
):
    s = lax.axis_index("section")
    t = lax.axis_index("tp")
    y, j = s // 4, s % 4
    lo, c = j // 2, j % 2
    down = lax.all_gather(adapter_down_factor[0], "tp", axis=0, tiled=True)
    kg, vg, back, qg4, hid4, wg = first_call(
        saved_queries[0],
        saved_keys[0],
        values[0],
        attention_output_grad[0],
        segments[:, None],
        segments[None, :],
        adapter_up_factor[0],
        hidden[0],
        shared_query_weight,
    )
    group = lax.dynamic_slice_in_dim(section_block_index[:, 0], y * 4, 4)
    ids = jnp.concatenate([group, c[None].astype(group.dtype)])
    partial = input_grad_call(ids, qg4, wg)
    summed = lax.psum_scatter(
        partial.reshape(NTP * 160, 2 * COLS), "tp", scatter_dimension=0, tiled=True
    ).reshape(5, 32, 2 * COLS)

    start = 896 * lo + 384 * c
    emb = jnp.stack(
        [lax.dynamic_slice_in_dim(embedding, start + 1792 * part, WIN, 1) for part in range(2)]
    )
    dw = weight_grad_call(ids, qg4, hid4, emb)
    back_rank = back.reshape(TOKENS, RANK)
    adapter = dot_nt(lax.dynamic_index_in_dim(back, t, keepdims=False), down)
    base = residual[0].astype(F32) + adapter[:, :WIDTH]
    adapter_embed = jnp.transpose(adapter[:, WIDTH:].reshape(32, NSEC, HD), (1, 0, 2))
    weight_grad, embed_part, next_base = second_call(dw, adapter_embed, base)

    qg = lax.dynamic_index_in_dim(qg4, j, keepdims=False)
    low_rank = (
        dot_nn(hidden[0], down[:WIDTH]) + dot_nn(embedding, down[WIDTH:])
    ).astype(BF16)
    up_grad = dot_tn(low_rank, qg)
    hidden_cols = lax.dynamic_slice_in_dim(hidden[0], (t % 8) * COLS, COLS, 1)
    embed_cols = lax.dynamic_slice_in_dim(embedding, (t % 8) * COLS, COLS, 1)
    down_grad = dot_tn(jnp.where(t < 8, hidden_cols, embed_cols), back_rank)

    emb_out = jnp.transpose(summed[4].reshape(32, 4, HD), (1, 0, 2))
    pland, eland = third_call(summed[:4], emb_out)
    moved = jnp.transpose(pland.reshape(4, 32, 2, COLS), (1, 2, 0, 3)).reshape(32, WIDTH)
    passed = jnp.where(s == NSEC - 1, 0.0, next_base + moved.astype(F32)).astype(BF16)
    embed_grad = embed_part + jnp.sum(eland.astype(F32), axis=0)
    return (
        kg[None],
        vg[None],
        down_grad[None],
        up_grad[None],
        weight_grad,
        passed[None],
        embed_grad,
    )


def solution(mesh):
    in_specs = (
        P("section", None, "tp"),
        P("section", None, "tp"),
        P("section", None, "tp"),
        P("section", None, "tp"),
        P(),
        P("section", None, None),
        P(),
        P(),
        P(None, "section", "tp"),
        P("section", "tp", None),
        P("section", None, "tp"),
        P("section", "tp", None),
    )
    out_specs = (
        P("section", None, "tp"),
        P("section", None, "tp"),
        P("section", "tp", None),
        P("section", None, "tp"),
        P(None, "section", "tp"),
        P("section", "tp", None),
        P("tp", "section"),
    )
    return jax.shard_map(
        on_device, mesh=mesh, in_specs=in_specs, out_specs=out_specs, check_vma=False
    )
```

```python
import jax
import jax.numpy as jnp
from jax import lax
from jax.experimental import pallas as pl
from jax.experimental.pallas import tpu as pltpu
from jax.sharding import PartitionSpec as P

MESH = pl.DeviceIdType.MESH
TOKENS = 512
WIDTH = 3584
COLS = 448
HD = 224
RANK = 128
WIN = 512
NSEC = 16
NTP = 16
SPLIT = 128
STEPS = 7
PARTS = 5
VMEM_LIMIT = 60 * 1024 * 1024
F32 = jnp.float32
BF16 = jnp.bfloat16


def dot_nt(a, b):
    return lax.dot_general(a, b, (((1,), (1,)), ((), ())), preferred_element_type=F32)


def dot_tn(a, b):
    return lax.dot_general(a, b, (((0,), (0,)), ((), ())), preferred_element_type=F32)


def dot_nn(a, b):
    return lax.dot_general(a, b, (((1,), (0,)), ((), ())), preferred_element_type=F32)


def remote(src, dst, send_sem, recv_sem, section, tp):
    return pltpu.make_async_remote_copy(
        src_ref=src,
        dst_ref=dst,
        send_sem=send_sem,
        recv_sem=recv_sem,
        device_id={"section": section, "tp": tp},
        device_id_type=MESH,
    )


def greet(peers):
    barrier = pltpu.get_barrier_semaphore()
    for section, tp in peers:
        pl.semaphore_signal(
            barrier, inc=1, device_id={"section": section, "tp": tp}, device_id_type=MESH
        )
    pl.semaphore_wait(barrier, len(peers))


def attention(q_ref, k_ref, v_ref, g_ref, seg_ref, qg, qgt, kg_ref, vg_ref):
    scale = HD ** (-0.5)
    seg_col = jnp.transpose(jnp.broadcast_to(seg_ref[...], (RANK, TOKENS)))[:, 0:1]
    key_id = lax.broadcasted_iota(jnp.int32, (TOKENS, TOKENS), 0)
    query_id = lax.broadcasted_iota(jnp.int32, (TOKENS, TOKENS), 1)
    allowed = (key_id <= query_id) & (seg_col == seg_ref[...])
    for head in range(2):
        rows = pl.ds(head * HD, HD)
        q, k, v, g = q_ref[rows, :], k_ref[rows, :], v_ref[rows, :], g_ref[rows, :]
        scores = jnp.where(allowed, dot_tn(k, q) * scale, -1e30)
        expo = jnp.exp(scores - jnp.max(scores, axis=0, keepdims=True))
        probs = expo / jnp.sum(expo, axis=0, keepdims=True)
        low = probs.astype(BF16)
        grad = dot_tn(v, g)
        delta = jnp.sum(low.astype(F32) * grad, axis=0, keepdims=True)
        dscore = (probs * (grad - delta)).astype(BF16)
        dq = (dot_nn(k, dscore) * scale).astype(BF16)
        qgt[rows, :] = dq
        qg[:, rows] = jnp.transpose(dq)
        kg_ref[rows, :] = (dot_nt(q, dscore) * scale).astype(BF16)
        vg_ref[rows, :] = dot_nt(g, low).astype(BF16)


def whole_kernel(
    ids, q_ref, k_ref, v_ref, g_ref, seg_ref, upt_ref, down_ref, hidden, embedding, weight, residual,
    kg_ref, vg_ref, dg_ref, ugt_ref, wsum_ref, pland, eland, next_res,
    qg, qgt, qg4, hid4, wg, embw, jw, adp, adw, bgrp, bpart, bland, bown, ball,
    partial, ring, hland, total, etotal, fbuf, qb, acc, dws, dwl,
    loc_sem, ws_sem, wr_sem, hs_sem, hr_sem, qs_sem, qr_sem, bs_sem, br_sem, cs_sem, cr_sem,
    ds_sem, dr_sem, gs_sem, gr_sem, rs_sem, rr_sem, is_sem, ir_sem, xs_sem, xr_sem,
    ps_sem, pr_sem, es_sem, er_sem, fin_sem, res_sem,
):
    s = lax.axis_index("section")
    t = lax.axis_index("tp")
    y, j = s // 4, s % 4
    lo, c = j // 2, j % 2
    hi, z = t // 8, t % 8
    sib = y * 4 + 2 * lo + (1 - c)
    across = [y * 4 + 2 * (1 - lo) + i for i in range(2)]
    partner = y * 4 + 2 * (1 - lo) + c
    t_far = (1 - hi) * 8 + z
    yl, yr, yo = (y + 3) % 4, (y + 1) % 4, (y + 2) % 4
    left, right = yl * 4 + j, yr * 4 + j
    z_next, z_prev = hi * 8 + (z + 1) % 8, hi * 8 + (z + 7) % 8
    tp_peers = [(t + i) % NTP for i in range(1, NTP)]
    section_peers = [(s + i) % NSEC for i in range(1, NSEC)]
    greet(
        [(p, t) for p in section_peers]
        + [(s, p) for p in tp_peers]
        + [(a, t_far) for a in across]
    )

    def row_block(b, owner_y):
        return wg.at[b, pl.ds(pl.multiple_of(owner_y * COLS, 64), COLS), :]

    def window(lo_d, c_d, part):
        return pl.ds(pl.multiple_of(896 * lo_d + 384 * c_d + 1792 * part, 128), WIN)

    wsends = []
    for n, (b, dest, slot) in enumerate([(0, right, 0), (1, left, 3), (1, right, 1), (0, left, 2)]):
        copy = remote(weight.at[b], row_block(b, y), ws_sem.at[n], wr_sem.at[slot], dest, t)
        copy.start()
        wsends.append(copy)

    hsends = []

    def send_hidden(part):
        for i in range(2):
            near = remote(
                hidden.at[pl.ds(0, SPLIT), window(1 - lo, i, part)],
                hid4.at[j, part, pl.ds(0, SPLIT), :],
                hs_sem.at[len(hsends)], hr_sem.at[2 + 2 * c + part], across[i], t,
            )
            near.start()
            hsends.append(near)
            far = remote(
                hidden.at[pl.ds(SPLIT, TOKENS - SPLIT), window(1 - lo, i, part)],
                hid4.at[j, part, pl.ds(SPLIT, TOKENS - SPLIT), :],
                hs_sem.at[len(hsends)], hr_sem.at[6 + 2 * c + part], across[i], t_far,
            )
            far.start()
            hsends.append(far)
        twin = remote(
            hidden.at[:, window(lo, 1 - c, part)], hid4.at[j, part],
            hs_sem.at[len(hsends)], hr_sem.at[part], sib, t,
        )
        twin.start()
        hsends.append(twin)

    locals_ = []

    def here(src, dst):
        copy = pltpu.make_async_copy(src, dst, loc_sem.at[len(locals_)])
        copy.start()
        locals_.append(copy)
        return copy

    jwin = pl.ds(pl.multiple_of(896 * (z // 2) + 384 * (z % 2), 128), WIN)
    from_hidden = pltpu.make_async_copy(hidden.at[:, jwin], jw, loc_sem.at[8])
    from_embedding = pltpu.make_async_copy(embedding.at[:, jwin], jw, loc_sem.at[8])

    @pl.when(t < 8)
    def _():
        from_hidden.start()

    @pl.when(t >= 8)
    def _():
        from_embedding.start()

    send_hidden(0)
    for b in range(2):
        here(weight.at[b], row_block(b, y))
    for part in range(2):
        here(hidden.at[:, window(lo, c, part)], hid4.at[j, part])
        here(embedding.at[:, window(lo, c, part)], embw.at[part])

    adder = t % 4
    half = (t // 4) % 2
    mine = pl.ds(pl.multiple_of(half * COLS, 64), COLS)
    other = pl.ds(pl.multiple_of((1 - half) * COLS, 64), COLS)
    down_copy = remote(down_ref, adw.at[j, mine, :], gs_sem.at[0], gr_sem.at[j], y * 4 + adder, t)
    back_copy = remote(
        ball.at[:, :, pl.ds(0, RANK)], bgrp.at[j], gs_sem.at[1], gr_sem.at[4 + j], y * 4 + adder, t
    )
    adw[:, other, :] = jnp.zeros((4, COLS, RANK), BF16)

    @pl.when(j != adder)
    def _():
        down_copy.start()

    @pl.when(j == adder)
    def _():
        adw[j, mine, :] = down_ref[...]

    res_copy = remote(
        residual, next_res, res_sem.at[0], res_sem.at[1], (s + NSEC - 1) % NSEC, t
    )
    res_copy.start()

    attention(q_ref, k_ref, v_ref, g_ref, seg_ref, qg, qgt, kg_ref, vg_ref)

    q_near = remote(qg, qg4.at[j], qs_sem.at[0], qr_sem.at[j], partner, t)
    q_near.start()
    q_twin = remote(qg, qg4.at[j], qs_sem.at[1], qr_sem.at[j], sib, t)
    q_twin.start()
    qg4[j] = qg[...]

    adp[...] = jnp.zeros_like(adp)
    adp[pl.ds(pl.multiple_of(64 * (z % 2), 64), COLS), :] = down_ref[...]
    bpart[:, :, 0:RANK] = dot_nn(qg[...], upt_ref[...]).reshape(NTP, 32, RANK)
    from_hidden.wait()
    bpart[:, :, RANK : 2 * RANK] = dot_nn(jw[...], adp[...]).reshape(NTP, 32, RANK)
    bsends = []
    for n, peer in enumerate(tp_peers):
        copy = remote(bpart.at[peer], bland.at[t], bs_sem.at[n], br_sem.at[t], s, peer)
        copy.start()
        bsends.append(copy)
    bland[t] = bpart[t]
    send_hidden(1)

    def wait_w(b, owner_y, slot):
        remote(weight.at[b], row_block(b, owner_y), ws_sem.at[0], wr_sem.at[slot], left, t).wait_recv()

    wait_w(0, yl, 0)
    copy = remote(row_block(0, yl), row_block(0, yl), ws_sem.at[4], wr_sem.at[4], right, t)
    copy.start()
    wsends.append(copy)
    wait_w(1, yr, 3)
    copy = remote(row_block(1, yr), row_block(1, yr), ws_sem.at[5], wr_sem.at[5], left, t)
    copy.start()
    wsends.append(copy)

    for peer in tp_peers:
        remote(bpart.at[peer], bland.at[peer], bs_sem.at[0], br_sem.at[peer], s, peer).wait_recv()
    bown[...] = jnp.sum(bland[...], axis=0).astype(BF16)
    csends = []
    for n, peer in enumerate(tp_peers):
        copy = remote(bown, ball.at[t], cs_sem.at[n], cr_sem.at[t], s, peer)
        copy.start()
        csends.append(copy)
    ball[t] = bown[...]

    def wait_q(slot):
        remote(qg, qg4.at[slot], qs_sem.at[0], qr_sem.at[slot], sib, t).wait_recv()

    slot_partner = 2 * (1 - lo) + c
    wait_q(slot_partner)
    q_on = remote(
        qg4.at[slot_partner], qg4.at[slot_partner], qs_sem.at[2], qr_sem.at[slot_partner], sib, t
    )
    q_on.start()

    for peer in tp_peers:
        remote(bown, ball.at[peer], cs_sem.at[0], cr_sem.at[peer], s, peer).wait_recv()

    @pl.when(j != adder)
    def _():
        back_copy.start()

    @pl.when(j == adder)
    def _():
        bgrp[j] = ball[:, :, 0:RANK]

    wait_q(2 * lo + 1 - c)
    wait_q(2 * (1 - lo) + 1 - c)

    def keep(n, b):
        return jnp.where(ids[4 * y + n] == b, 1.0, 0.0).astype(F32)

    for b in range(2):
        picked = qg4[0].astype(F32) * keep(0, b)
        for n in range(1, 4):
            picked = picked + qg4[n].astype(F32) * keep(n, b)
        qb[b] = picked.astype(BF16)

    @pl.when(j == adder)
    def _():
        for n in range(4):
            @pl.when(j != n)
            def _():
                remote(
                    down_ref, adw.at[n, mine, :], gs_sem.at[0], gr_sem.at[n], y * 4 + adder, t
                ).wait_recv()
                remote(
                    ball.at[:, :, pl.ds(0, RANK)], bgrp.at[n], gs_sem.at[1], gr_sem.at[4 + n], y * 4 + adder, t
                ).wait_recv()

    for copy in locals_:
        copy.wait()
    wait_w(1, yl, 1)
    wait_w(0, yr, 2)
    wait_w(0, yo, 4)
    wait_w(1, yo, 5)

    def chunk(d, k):
        return (z + 15 - k) % 8 if d == 0 else 8 + (z + 1 + k) % 8

    def hop(d, p, k):
        return remote(
            partial.at[chunk(d, k), p], ring.at[d, p, k],
            rs_sem.at[d, p, k], rr_sem.at[d, p, k], s, z_next if d == 0 else z_prev,
        )

    for p in range(PARTS):
        if p < 4:
            picked = wg[0, 0 : 2 * COLS, :] * keep(p, 0).astype(BF16) + wg[
                1, 0 : 2 * COLS, :
            ] * keep(p, 1).astype(BF16)
            fbuf[...] = dot_nt(qg4[p], picked)

            @pl.when((j == adder) & (t < 8))
            def _():
                fbuf[...] += dot_nt(bgrp[p].reshape(TOKENS, RANK), adw[p])
        else:
            fbuf[...] = dot_nt(qb[0], wg[0, 2 * COLS :, :]) + dot_nt(qb[1], wg[1, 2 * COLS :, :])

            @pl.when((j == adder) & (t >= 8))
            def _():
                for n in range(4):
                    fbuf[...] += dot_nt(bgrp[n].reshape(TOKENS, RANK), adw[n])

        partial[:, p] = fbuf[...].reshape(NTP, 32, 2 * COLS).astype(BF16)
        for d in range(2):
            hop(d, p, 0).start()

    for part in range(2):
        remote(
            hidden.at[:, window(lo, c, part)], hid4.at[2 * lo + 1 - c, part],
            hs_sem.at[0], hr_sem.at[part], sib, t,
        ).wait_recv()
        for i in range(2):
            for first, count, base in ((0, SPLIT, 2), (SPLIT, TOKENS - SPLIT, 6)):
                remote(
                    hidden.at[pl.ds(first, count), window(lo, c, part)],
                    hid4.at[2 * (1 - lo) + i, part, pl.ds(first, count), :],
                    hs_sem.at[0], hr_sem.at[base + 2 * i + part], sib, t,
                ).wait_recv()

    skip = pl.ds(pl.multiple_of(64 * c, 64), COLS)

    def weight_send(i, yd):
        return remote(dws.at[i], dwl.at[i], xs_sem.at[i], xr_sem.at[i], yd * 4 + j, t)

    def ring_step(k, carry):
        for p in range(PARTS):
            for d in range(2):
                hop(d, p, k - 1).wait_recv()
                partial[chunk(d, k), p] = (
                    partial[chunk(d, k), p].astype(F32) + ring[d, p, k - 1].astype(F32)
                ).astype(BF16)
                hop(d, p, k).start()

        @pl.when(k <= 4)
        def _():
            yd = (y + k) % 4

            @pl.when(yd < 2)
            def _():
                for n in range(4):
                    term = dot_tn(hid4[n, yd], qg4[n])
                    for b in range(2):
                        if n == 0:
                            acc[b] = term * keep(n, b)
                        else:
                            acc[b] += term * keep(n, b)

            @pl.when(yd >= 2)
            def _():
                for b in range(2):
                    acc[b] = dot_tn(embw[yd % 2], qb[b])

            for b in range(2):
                dws[k - 1, b] = acc[b, skip, :].astype(BF16)

            @pl.when(k < 4)
            def _():
                weight_send(k - 1, yd).start()

        return carry

    lax.fori_loop(1, STEPS, ring_step, 0)

    back = ball[:, :, 0:RANK].reshape(TOKENS, RANK)
    low = ball[:, :, RANK : 2 * RANK].reshape(TOKENS, RANK)
    ugt_ref[...] = dot_nn(qgt[...], low)
    fbuf[:, 0:RANK] = dot_tn(jw[...], back)
    dg_ref[...] = fbuf[pl.ds(pl.multiple_of(64 * (z % 2), 64), COLS), 0:RANK]

    def swap(p):
        return remote(
            partial.at[(1 - hi) * 8 + z, p], hland.at[p], is_sem.at[p], ir_sem.at[p], s, t_far
        )

    for p in range(PARTS):
        for d in range(2):
            hop(d, p, STEPS - 1).wait_recv()
            partial[chunk(d, STEPS), p] = (
                partial[chunk(d, STEPS), p].astype(F32) + ring[d, p, STEPS - 1].astype(F32)
            ).astype(BF16)
        swap(p).start()

    for i in range(3):
        weight_send(i, yl).wait_recv()
    for b in range(2):
        wsum_ref[b] = (
            dws[3, b].astype(F32) + dwl[0, b].astype(F32)
            + (dwl[1, b].astype(F32) + dwl[2, b].astype(F32))
        )

    def move(src, dst, send_sem, recv_sem, here_sem, dest):
        away = remote(src, dst, send_sem, recv_sem, dest, t)
        near = pltpu.make_async_copy(src, dst, here_sem)

        @pl.when(dest != s)
        def _():
            away.start()

        @pl.when(dest == s)
        def _():
            near.start()

        def finish():
            @pl.when(dest != s)
            def _():
                away.wait_send()

            @pl.when(dest == s)
            def _():
                near.wait()

        return finish

    ends = []
    for p in range(PARTS):
        swap(p).wait_recv()
        value = partial[hi * 8 + z, p].astype(F32) + hland[p].astype(F32)
        if p < 4:
            total[p] = value.astype(BF16)
            dest = (y * 4 + p + NSEC - 1) % NSEC
            ends.append(
                move(total.at[p], pland.at[j], ps_sem.at[p], pr_sem.at[j], fin_sem.at[p], dest)
            )
        else:
            for n in range(4):
                etotal[n] = value[:, n * HD : (n + 1) * HD]
                dest = 2 * j + n % 2 + 8 * (n // 2)
                ends.append(
                    move(etotal.at[n], eland.at[y], es_sem.at[n], er_sem.at[y], fin_sem.at[4 + n], dest)
                )

    for n in range(4):
        source = (((s + 1) % NSEC) // 4) * 4 + n

        @pl.when(source != s)
        def _():
            remote(total.at[n], pland.at[n], ps_sem.at[n], pr_sem.at[n], source, t).wait_recv()

    for n in range(4):
        source = n * 4 + (s % 8) // 2

        @pl.when(source != s)
        def _():
            remote(etotal.at[n], eland.at[n], es_sem.at[n], er_sem.at[n], source, t).wait_recv()

    for end in ends:
        end()
    res_copy.wait()
    for copy in wsends + hsends + bsends + csends + [q_near, q_twin, q_on]:
        copy.wait_send()

    @pl.when(j != adder)
    def _():
        down_copy.wait_send()
        back_copy.wait_send()

    def drain(k, carry):
        for p in range(PARTS):
            for d in range(2):
                hop(d, p, k).wait_send()
        return carry

    lax.fori_loop(0, STEPS, drain, 0)
    for p in range(PARTS):
        swap(p).wait_send()
    for i in range(3):
        weight_send(i, yl).wait_send()


def whole_call(ids, q, k, v, g, seg, upt, down, hidden, embedding, weight, residual):
    vm = pl.BlockSpec(memory_space=pltpu.VMEM)
    sm = pl.BlockSpec(memory_space=pltpu.SMEM)
    anys = pl.BlockSpec(memory_space=pl.ANY)
    dma = pltpu.SemaphoreType.DMA
    out = jax.ShapeDtypeStruct
    return pl.pallas_call(
        whole_kernel,
        out_shape=(
            out((COLS, TOKENS), BF16),
            out((COLS, TOKENS), BF16),
            out((COLS, RANK), F32),
            out((COLS, RANK), F32),
            out((2, COLS, COLS), F32),
            out((4, 32, 2 * COLS), BF16),
            out((4, 32, HD), F32),
            out((32, WIDTH), BF16),
        ),
        in_specs=[sm] + [vm] * 7 + [anys] * 4,
        out_specs=(vm, vm, vm, vm, vm, anys, anys, anys),
        scratch_shapes=[
            pltpu.VMEM((TOKENS, COLS), BF16),
            pltpu.VMEM((COLS, TOKENS), BF16),
            pltpu.VMEM((4, TOKENS, COLS), BF16),
            pltpu.VMEM((4, 2, TOKENS, WIN), BF16),
            pltpu.VMEM((2, 4 * COLS, COLS), BF16),
            pltpu.VMEM((2, TOKENS, WIN), BF16),
            pltpu.VMEM((TOKENS, WIN), BF16),
            pltpu.VMEM((WIN, RANK), BF16),
            pltpu.VMEM((4, 2 * COLS, RANK), BF16),
            pltpu.VMEM((4, NTP, 32, RANK), BF16),
            pltpu.VMEM((NTP, 32, 2 * RANK), F32),
            pltpu.VMEM((NTP, 32, 2 * RANK), F32),
            pltpu.VMEM((32, 2 * RANK), BF16),
            pltpu.VMEM((NTP, 32, 2 * RANK), BF16),
            pltpu.VMEM((NTP, PARTS, 32, 2 * COLS), BF16),
            pltpu.VMEM((2, PARTS, STEPS, 32, 2 * COLS), BF16),
            pltpu.VMEM((PARTS, 32, 2 * COLS), BF16),
            pltpu.VMEM((4, 32, 2 * COLS), BF16),
            pltpu.VMEM((4, 32, HD), F32),
            pltpu.VMEM((TOKENS, 2 * COLS), F32),
            pltpu.VMEM((2, TOKENS, COLS), BF16),
            pltpu.VMEM((2, WIN, COLS), F32),
            pltpu.VMEM((4, 2, COLS, COLS), BF16),
            pltpu.VMEM((3, 2, COLS, COLS), BF16),
            dma((9,)), dma((6,)), dma((6,)), dma((10,)), dma((10,)), dma((3,)), dma((4,)),
            dma((15,)), dma((16,)), dma((15,)), dma((16,)),
            dma((1,)), dma((1,)), dma((2,)), dma((8,)),
            dma((2, PARTS, STEPS)), dma((2, PARTS, STEPS)),
            dma((PARTS,)), dma((PARTS,)), dma((3,)), dma((3,)),
            dma((4,)), dma((4,)), dma((4,)), dma((4,)), dma((8,)), dma((2,)),
        ],
        compiler_params=pltpu.CompilerParams(
            collective_id=0, has_side_effects=True, vmem_limit_bytes=VMEM_LIMIT
        ),
        name="attention_block_backward",
    )(ids, q, k, v, g, seg, upt, down, hidden, embedding, weight, residual)


def on_device(
    saved_queries,
    saved_keys,
    values,
    attention_output_grad,
    segments,
    hidden,
    embedding,
    section_block_index,
    shared_query_weight,
    adapter_down_factor,
    adapter_up_factor,
    residual,
):
    s = lax.axis_index("section")
    kgt, vgt, down_grad, ugt, weight_grad, pland, eland, next_res = whole_call(
        section_block_index[:, 0],
        saved_queries[0].T,
        saved_keys[0].T,
        values[0].T,
        attention_output_grad[0].T,
        segments[None, :],
        adapter_up_factor[0].T,
        adapter_down_factor[0],
        hidden[0],
        embedding,
        shared_query_weight,
        residual[0],
    )
    moved = jnp.transpose(pland.reshape(4, 32, 2, COLS), (1, 2, 0, 3)).reshape(32, WIDTH)
    passed = jnp.where(
        s == NSEC - 1, 0.0, next_res.astype(F32) + moved.astype(F32)
    ).astype(BF16)
    return (
        kgt.T[None],
        vgt.T[None],
        down_grad[None],
        ugt.T[None],
        weight_grad,
        passed[None],
        jnp.sum(eland, axis=0),
    )


def solution(mesh):
    in_specs = (
        P("section", None, "tp"),
        P("section", None, "tp"),
        P("section", None, "tp"),
        P("section", None, "tp"),
        P(),
        P("section", None, None),
        P(),
        P(),
        P(None, "section", "tp"),
        P("section", "tp", None),
        P("section", None, "tp"),
        P("section", "tp", None),
    )
    out_specs = (
        P("section", None, "tp"),
        P("section", None, "tp"),
        P("section", "tp", None),
        P("section", None, "tp"),
        P(None, "section", "tp"),
        P("section", "tp", None),
        P("tp", "section"),
    )
    return jax.shard_map(
        on_device, mesh=mesh, in_specs=in_specs, out_specs=out_specs, check_vma=False
    )
```

```python
import jax
import jax.numpy as jnp
from jax import lax
from jax.experimental import pallas as pl
from jax.experimental.pallas import tpu as pltpu
from jax.sharding import PartitionSpec as P

MESH = pl.DeviceIdType.MESH
TOKENS = 512
WIDTH = 3584
COLS = 448
HD = 224
RANK = 128
WIN = 512
NSEC = 16
NTP = 16
SPLIT = 192
STEPS = 7
HALF = 224
PARTS = 5
VMEM_LIMIT = 60 * 1024 * 1024
F32 = jnp.float32
BF16 = jnp.bfloat16


def dot_nt(a, b):
    return lax.dot_general(a, b, (((1,), (1,)), ((), ())), preferred_element_type=F32)


def dot_tn(a, b):
    return lax.dot_general(a, b, (((0,), (0,)), ((), ())), preferred_element_type=F32)


def dot_nn(a, b):
    return lax.dot_general(a, b, (((1,), (0,)), ((), ())), preferred_element_type=F32)


def remote(src, dst, send_sem, recv_sem, section, tp):
    return pltpu.make_async_remote_copy(
        src_ref=src,
        dst_ref=dst,
        send_sem=send_sem,
        recv_sem=recv_sem,
        device_id={"section": section, "tp": tp},
        device_id_type=MESH,
    )


def greet(peers):
    barrier = pltpu.get_barrier_semaphore()
    for section, tp in peers:
        pl.semaphore_signal(
            barrier, inc=1, device_id={"section": section, "tp": tp}, device_id_type=MESH
        )
    pl.semaphore_wait(barrier, len(peers))


def attention(q_ref, k_ref, v_ref, g_ref, seg_ref, qg, qgt, kg_ref, vg_ref):
    scale = HD ** (-0.5)
    seg_col = jnp.transpose(jnp.broadcast_to(seg_ref[...], (RANK, TOKENS)))[:, 0:1]
    key_id = lax.broadcasted_iota(jnp.int32, (TOKENS, TOKENS), 0)
    query_id = lax.broadcasted_iota(jnp.int32, (TOKENS, TOKENS), 1)
    allowed = (key_id <= query_id) & (seg_col == seg_ref[...])
    for head in range(2):
        rows = pl.ds(head * HD, HD)
        q, k, v, g = q_ref[rows, :], k_ref[rows, :], v_ref[rows, :], g_ref[rows, :]
        scores = jnp.where(allowed, dot_tn(k, q) * scale, -1e30)
        expo = jnp.exp(scores - jnp.max(scores, axis=0, keepdims=True))
        probs = expo / jnp.sum(expo, axis=0, keepdims=True)
        low = probs.astype(BF16)
        grad = dot_tn(v, g)
        delta = jnp.sum(low.astype(F32) * grad, axis=0, keepdims=True)
        dscore = (probs * (grad - delta)).astype(BF16)
        dq = (dot_nn(k, dscore) * scale).astype(BF16)
        qgt[rows, :] = dq
        qg[:, rows] = jnp.transpose(dq)
        kg_ref[rows, :] = (dot_nt(q, dscore) * scale).astype(BF16)
        vg_ref[rows, :] = dot_nt(g, low).astype(BF16)


def whole_kernel(
    ids, q_ref, k_ref, v_ref, g_ref, seg_ref, upt_ref, down_ref, res_ref, hidden, embedding, weight,
    kg_ref, vg_ref, dg_ref, ugt_ref, wsum_ref, passed_ref, embed_ref,
    qg, qgt, qg4, hid4, wg, embw, jw, adp, dfull, bpart, bland, bown, ball,
    partial, ring, hland, total, etotal, pland, eland, nsend, nland, apsend, apland, fbuf, qb, acc, dws, dwl,
    loc_sem, ws_sem, wr_sem, hs_sem, hr_sem, qs_sem, qr_sem, bs_sem, br_sem, cs_sem, cr_sem,
    ds_sem, dr_sem, rs_sem, rr_sem, is_sem, ir_sem, xs_sem, xr_sem,
    ps_sem, pr_sem, es_sem, er_sem, fin_sem, ns_sem, as_sem, ar_sem,
):
    s = lax.axis_index("section")
    t = lax.axis_index("tp")
    y, j = s // 4, s % 4
    lo, c = j // 2, j % 2
    hi, z = t // 8, t % 8
    sib = y * 4 + 2 * lo + (1 - c)
    across = [y * 4 + 2 * (1 - lo) + i for i in range(2)]
    partner = y * 4 + 2 * (1 - lo) + c
    t_far = (1 - hi) * 8 + z
    yl, yr, yo = (y + 3) % 4, (y + 1) % 4, (y + 2) % 4
    left, right = yl * 4 + j, yr * 4 + j
    yin, yout = y + 1 - 2 * (y % 2), 3 - y
    z_next, z_prev = hi * 8 + (z + 1) % 8, hi * 8 + (z + 7) % 8
    tp_peers = [(t + i) % NTP for i in range(1, NTP)]
    section_peers = [(s + i) % NSEC for i in range(1, NSEC)]
    greet(
        [(p, t) for p in section_peers]
        + [(s, p) for p in tp_peers]
        + [(a, t_far) for a in across]
    )
    sent = []

    def go(copy):
        copy.start()
        sent.append(copy)
        return copy

    def piece(i, owner_y):
        first = pl.multiple_of(owner_y * COLS + HALF * (i % 2), 32)
        return wg.at[i // 2, pl.ds(first, HALF), :]

    def w_own(i, to_in):
        n = 4 * to_in + i
        return remote(
            weight.at[i // 2, pl.ds(HALF * (i % 2), HALF), :], piece(i, y),
            ws_sem.at[n], wr_sem.at[n], (yin if to_in else yout) * 4 + j, t,
        )

    def w_on(i):
        return remote(
            piece(i, yout), piece(i, yout), ws_sem.at[8 + i], wr_sem.at[8 + i], yin * 4 + j, t
        )

    def w_wait(kind, i):
        owner = (yout, yin, 3 - yin)[kind]
        n = 4 * kind + i
        remote(piece(i, owner), piece(i, owner), ws_sem.at[0], wr_sem.at[n], yin * 4 + j, t).wait_recv()

    @pl.when(y < 2)
    def _():
        for i in range(4):
            w_own(i, 1).start()

    for i in range(4):
        go(w_own(i, 0))

    def z_at(step):
        return (z + step + 8) % 8

    def d_send(n, slot, to):
        return remote(dfull.at[slot], dfull.at[slot], ds_sem.at[n], dr_sem.at[slot], s, to)

    def d_wait(slot):
        d_send(0, slot, t_far).wait_recv()

    dfull[t] = down_ref[...]
    for n, to in enumerate([t_far] + [hi * 8 + z_at(i) for i in (1, -1, 2, -2)]):
        go(d_send(n, t, to))

    def window(lo_d, c_d, part):
        return pl.ds(pl.multiple_of(896 * lo_d + 384 * c_d + 1792 * part, 128), WIN)

    def send_hidden(part):
        n = 5 * part
        for i in range(2):
            go(remote(
                hidden.at[pl.ds(0, SPLIT), window(1 - lo, i, part)],
                hid4.at[j, part, pl.ds(0, SPLIT), :],
                hs_sem.at[n + 2 * i], hr_sem.at[2 + 2 * c + part], across[i], t,
            ))
            go(remote(
                hidden.at[pl.ds(SPLIT, TOKENS - SPLIT), window(1 - lo, i, part)],
                hid4.at[j, part, pl.ds(SPLIT, TOKENS - SPLIT), :],
                hs_sem.at[n + 2 * i + 1], hr_sem.at[6 + 2 * c + part], across[i], t_far,
            ))
        go(remote(
            hidden.at[:, window(lo, 1 - c, part)], hid4.at[j, part],
            hs_sem.at[n + 4], hr_sem.at[part], sib, t,
        ))

    locals_ = []

    def here(src, dst):
        copy = pltpu.make_async_copy(src, dst, loc_sem.at[len(locals_)])
        copy.start()
        locals_.append(copy)

    jwin = pl.ds(pl.multiple_of(896 * (z // 2) + 384 * (z % 2), 128), WIN)
    from_hidden = pltpu.make_async_copy(hidden.at[:, jwin], jw, loc_sem.at[8])
    from_embedding = pltpu.make_async_copy(embedding.at[:, jwin], jw, loc_sem.at[8])

    @pl.when(t < 8)
    def _():
        from_hidden.start()

    @pl.when(t >= 8)
    def _():
        from_embedding.start()

    send_hidden(0)
    for b in range(2):
        here(weight.at[b], wg.at[b, pl.ds(pl.multiple_of(y * COLS, 64), COLS), :])
    for part in range(2):
        here(hidden.at[:, window(lo, c, part)], hid4.at[j, part])
        here(embedding.at[:, window(lo, c, part)], embw.at[part])

    attention(q_ref, k_ref, v_ref, g_ref, seg_ref, qg, qgt, kg_ref, vg_ref)

    go(remote(qg, qg4.at[j], qs_sem.at[0], qr_sem.at[j], partner, t))
    go(remote(qg, qg4.at[j], qs_sem.at[1], qr_sem.at[j], sib, t))
    qg4[j] = qg[...]

    w_wait(0, 0)
    go(w_on(0))

    d_wait(t_far)
    for n, to in enumerate([hi * 8 + z_at(i) for i in (1, -1, 2, -2)]):
        go(d_send(5 + n, t_far, to))

    adp[...] = jnp.zeros_like(adp)
    adp[pl.ds(pl.multiple_of(64 * (z % 2), 64), COLS), :] = down_ref[...]
    bpart[:, :, 0:RANK] = dot_nn(qg[...], upt_ref[...]).reshape(NTP, 32, RANK)
    from_hidden.wait()
    bpart[:, :, RANK : 2 * RANK] = dot_nn(jw[...], adp[...]).reshape(NTP, 32, RANK)
    for n, peer in enumerate(tp_peers):
        go(remote(bpart.at[peer], bland.at[t], bs_sem.at[n], br_sem.at[t], s, peer))
    bland[t] = bpart[t]

    w_wait(0, 1)
    go(w_on(1))
    send_hidden(1)

    def wait_q(slot):
        remote(qg, qg4.at[slot], qs_sem.at[0], qr_sem.at[slot], sib, t).wait_recv()

    w_wait(0, 2)
    go(w_on(2))
    slot_partner = 2 * (1 - lo) + c
    wait_q(slot_partner)
    go(remote(
        qg4.at[slot_partner], qg4.at[slot_partner], qs_sem.at[2], qr_sem.at[slot_partner], sib, t
    ))

    for m, other in enumerate((t, t_far)):
        base = other - z
        down2, up2 = base + z_at(-2), base + z_at(2)
        d_wait(down2)
        d_wait(up2)
        to = t - z
        go(d_send(9 + 3 * m, down2, to + z_at(1)))
        go(d_send(10 + 3 * m, down2, to + z_at(2)))
        go(d_send(11 + 3 * m, up2, to + z_at(-1)))

    w_wait(0, 3)
    go(w_on(3))

    @pl.when(y >= 2)
    def _():
        for i in range(4):
            w_own(i, 1).start()

    wait_q(2 * lo + 1 - c)
    wait_q(2 * (1 - lo) + 1 - c)

    def keep(n, b):
        return jnp.where(ids[4 * y + n] == b, 1.0, 0.0).astype(F32)

    for b in range(2):
        picked = qg4[0].astype(F32) * keep(0, b)
        for n in range(1, 4):
            picked = picked + qg4[n].astype(F32) * keep(n, b)
        qb[b] = picked.astype(BF16)
    for copy in locals_:
        copy.wait()

    @pl.when(y < 2)
    def _():
        for i in range(4):
            w_wait(1, i)

    @pl.when(y >= 2)
    def _():
        for i in range(4):
            w_wait(2, i)

    def chunk(d, k):
        return (z + 15 - k) % 8 if d == 0 else 8 + (z + 1 + k) % 8

    def hop(d, p, k):
        return remote(
            partial.at[chunk(d, k), p], ring.at[d, p, k],
            rs_sem.at[d, p, k], rr_sem.at[d, p, k], s, z_next if d == 0 else z_prev,
        )

    def store(p, value):
        partial[:, p] = value.reshape(NTP, 32, 2 * COLS).astype(BF16)
        for d in range(2):
            go(hop(d, p, 0))

    def advance(p, k):
        for d in range(2):
            hop(d, p, k - 1).wait_recv()
            partial[chunk(d, k), p] = (
                partial[chunk(d, k), p].astype(F32) + ring[d, p, k - 1].astype(F32)
            ).astype(BF16)
            if k < STEPS:
                go(hop(d, p, k))

    for p in range(4):
        picked = wg[0, 0 : 2 * COLS, :] * keep(p, 0).astype(BF16) + wg[
            1, 0 : 2 * COLS, :
        ] * keep(p, 1).astype(BF16)
        store(p, dot_nt(qg4[p], picked))

    def sum_low_rank():
        for peer in tp_peers:
            remote(bpart.at[peer], bland.at[peer], bs_sem.at[0], br_sem.at[peer], s, peer).wait_recv()
        bown[...] = jnp.sum(bland[...], axis=0).astype(BF16)
        for n, peer in enumerate(tp_peers):
            go(remote(bown, ball.at[t], cs_sem.at[n], cr_sem.at[t], s, peer))
        ball[t] = bown[...]

    def wait_hidden():
        for part in range(2):
            remote(
                hidden.at[:, window(lo, c, part)], hid4.at[2 * lo + 1 - c, part],
                hs_sem.at[0], hr_sem.at[part], sib, t,
            ).wait_recv()
            for i in range(2):
                for first, count, base in ((0, SPLIT, 2), (SPLIT, TOKENS - SPLIT, 6)):
                    remote(
                        hidden.at[pl.ds(first, count), window(lo, c, part)],
                        hid4.at[2 * (1 - lo) + i, part, pl.ds(first, count), :],
                        hs_sem.at[0], hr_sem.at[base + 2 * i + part], sib, t,
                    ).wait_recv()

    skip = pl.ds(pl.multiple_of(64 * c, 64), COLS)

    def weight_rows(yd):
        @pl.when(yd < 2)
        def _():
            for n in range(4):
                term = dot_tn(hid4[n, yd % 2], qg4[n])
                for b in range(2):
                    if n == 0:
                        acc[b] = term * keep(n, b)
                    else:
                        acc[b] += term * keep(n, b)

        @pl.when(yd >= 2)
        def _():
            for b in range(2):
                acc[b] = dot_tn(embw[yd % 2], qb[b])

    def x_copy(n):
        to_right = n in (0, 2, 3)
        return remote(dws.at[n], dwl.at[n], xs_sem.at[n], xr_sem.at[n], right if to_right else left, t)

    def weight_far():
        weight_rows(yo)
        for b in range(2):
            dws[b] = acc[b, skip, :].astype(BF16)
            go(x_copy(b))

    def weight_near(side):
        weight_rows((yr, yl)[side])
        base = 2 + 2 * side
        dws[base + 1 - side] = acc[1 - side, skip, :].astype(BF16)
        go(x_copy(base + 1 - side))
        x_copy(side).wait_recv()
        dws[base + side] = (acc[side, skip, :] + dwl[side].astype(F32)).astype(BF16)
        go(x_copy(base + side))

    def weight_own():
        weight_rows(y)

    def embed_part():
        @pl.when(y < 2)
        def _():
            for i in range(4):
                w_wait(2, i)

        @pl.when(y >= 2)
        def _():
            for i in range(4):
                w_wait(1, i)

        store(4, dot_nt(qb[0], wg[0, 2 * COLS :, :]) + dot_nt(qb[1], wg[1, 2 * COLS :, :]))

    def n_copy():
        return remote(nsend, nland, ns_sem.at[0], ns_sem.at[1], (s + NSEC - 1) % NSEC, t)

    def adapter_term():
        for i in range(1, 8):
            d_wait(hi * 8 + z_at(i)) if i not in (2, 6) else None
            d_wait((1 - hi) * 8 + z_at(i)) if i not in (2, 6) else None
        own = bown[:, 0:RANK]
        residual = res_ref[...].astype(F32)
        for n in range(NTP):
            term = dot_nt(own, dfull[n])
            if n < 8:
                nsend[n] = (residual[:, n * COLS : (n + 1) * COLS] + term).astype(BF16)
            else:
                for h in range(2):
                    apsend[2 * (n - 8) + h] = term[:, h * HD : (h + 1) * HD]
        go(n_copy())
        for n, peer in enumerate(section_peers):
            go(remote(apsend.at[peer], apland.at[s], as_sem.at[n], ar_sem.at[s], peer, t))
        apland[s] = apsend[s]

    for k in range(1, STEPS):
        for p in range(4):
            advance(p, k)
        if k == 1:
            sum_low_rank()
        if k == 2:
            wait_hidden()
            weight_far()
        if k == 3:
            embed_part()
            weight_near(0)
        if k == 4:
            advance(4, 1)
            weight_near(1)
        if k == 5:
            advance(4, 2)
            weight_own()
        if k == 6:
            advance(4, 3)
            adapter_term()

    def swap(p):
        return remote(
            partial.at[(1 - hi) * 8 + z, p], hland.at[p], is_sem.at[p], ir_sem.at[p], s, t_far
        )

    def move(src, dst, send_sem, recv_sem, here_sem, dest):
        away = remote(src, dst, send_sem, recv_sem, dest, t)
        near = pltpu.make_async_copy(src, dst, here_sem)

        @pl.when(dest != s)
        def _():
            away.start()

        @pl.when(dest == s)
        def _():
            near.start()

        def finish():
            @pl.when(dest != s)
            def _():
                away.wait_send()

            @pl.when(dest == s)
            def _():
                near.wait()

        return finish

    ends = []

    def joined_halves(p):
        swap(p).wait_recv()
        return partial[hi * 8 + z, p].astype(F32) + hland[p].astype(F32)

    for p in range(4):
        advance(p, STEPS)
        go(swap(p))
    advance(4, 4)
    for peer in tp_peers:
        remote(bown, ball.at[peer], cs_sem.at[0], cr_sem.at[peer], s, peer).wait_recv()
    ugt_ref[...] = dot_nn(qgt[...], ball[:, :, RANK : 2 * RANK].reshape(TOKENS, RANK))
    advance(4, 5)
    for p in range(4):
        total[p] = joined_halves(p).astype(BF16)
        dest = (y * 4 + p + NSEC - 1) % NSEC
        ends.append(move(total.at[p], pland.at[j], ps_sem.at[p], pr_sem.at[j], fin_sem.at[p], dest))
    advance(4, 6)
    fbuf[...] = dot_tn(jw[...], ball[:, :, 0:RANK].reshape(TOKENS, RANK))
    dg_ref[...] = fbuf[pl.ds(pl.multiple_of(64 * (z % 2), 64), COLS), :]
    for n in (2, 3, 4, 5):
        x_copy(n).wait_recv()
    for b in range(2):
        wsum_ref[b] = acc[b, skip, :] + (dwl[2 + b].astype(F32) + dwl[4 + b].astype(F32))
    advance(4, STEPS)
    go(swap(4))

    n_copy().wait_recv()
    for n in range(4):
        source = (((s + 1) % NSEC) // 4) * 4 + n

        @pl.when(source != s)
        def _():
            remote(total.at[n], pland.at[n], ps_sem.at[n], pr_sem.at[n], source, t).wait_recv()

    value = joined_halves(4)
    for n in range(4):
        etotal[n] = value[:, n * HD : (n + 1) * HD]
        dest = 2 * j + n % 2 + 8 * (n // 2)
        ends.append(
            move(etotal.at[n], eland.at[y], es_sem.at[n], er_sem.at[y], fin_sem.at[4 + n], dest)
        )
    for end in ends:
        end()
    more = jnp.where(s == NSEC - 1, 0.0, 1.0).astype(F32)
    for n in range(8):
        half = pland[n % 4].astype(F32)[:, (n // 4) * COLS : (n // 4 + 1) * COLS]
        passed_ref[:, n * COLS : (n + 1) * COLS] = (
            (nland[n].astype(F32) + half) * more
        ).astype(BF16)
    for peer in section_peers:
        remote(apsend.at[peer], apland.at[peer], as_sem.at[0], ar_sem.at[peer], peer, t).wait_recv()
    for n in range(4):
        source = n * 4 + (s % 8) // 2

        @pl.when(source != s)
        def _():
            remote(etotal.at[n], eland.at[n], es_sem.at[n], er_sem.at[n], source, t).wait_recv()

    embed_ref[...] = jnp.sum(eland[...], axis=0) + jnp.sum(apland[...], axis=0)
    for copy in sent:
        copy.wait_send()
    for i in range(4):
        w_own(i, 1).wait_send()


def whole_call(ids, q, k, v, g, seg, upt, down, residual, hidden, embedding, weight):
    vm = pl.BlockSpec(memory_space=pltpu.VMEM)
    sm = pl.BlockSpec(memory_space=pltpu.SMEM)
    anys = pl.BlockSpec(memory_space=pl.ANY)
    dma = pltpu.SemaphoreType.DMA
    out = jax.ShapeDtypeStruct
    return pl.pallas_call(
        whole_kernel,
        out_shape=(
            out((COLS, TOKENS), BF16),
            out((COLS, TOKENS), BF16),
            out((COLS, RANK), F32),
            out((COLS, RANK), F32),
            out((2, COLS, COLS), F32),
            out((32, WIDTH), BF16),
            out((32, HD), F32),
        ),
        in_specs=[sm] + [vm] * 8 + [anys] * 3,
        out_specs=(vm,) * 7,
        scratch_shapes=[
            pltpu.VMEM((TOKENS, COLS), BF16),
            pltpu.VMEM((COLS, TOKENS), BF16),
            pltpu.VMEM((4, TOKENS, COLS), BF16),
            pltpu.VMEM((4, 2, TOKENS, WIN), BF16),
            pltpu.VMEM((2, 4 * COLS, COLS), BF16),
            pltpu.VMEM((2, TOKENS, WIN), BF16),
            pltpu.VMEM((TOKENS, WIN), BF16),
            pltpu.VMEM((WIN, RANK), BF16),
            pltpu.VMEM((NTP, COLS, RANK), BF16),
            pltpu.VMEM((NTP, 32, 2 * RANK), F32),
            pltpu.VMEM((NTP, 32, 2 * RANK), F32),
            pltpu.VMEM((32, 2 * RANK), BF16),
            pltpu.VMEM((NTP, 32, 2 * RANK), BF16),
            pltpu.VMEM((NTP, PARTS, 32, 2 * COLS), BF16),
            pltpu.VMEM((2, PARTS, STEPS, 32, 2 * COLS), BF16),
            pltpu.VMEM((PARTS, 32, 2 * COLS), BF16),
            pltpu.VMEM((4, 32, 2 * COLS), BF16),
            pltpu.VMEM((4, 32, HD), F32),
            pltpu.VMEM((4, 32, 2 * COLS), BF16),
            pltpu.VMEM((4, 32, HD), F32),
            pltpu.VMEM((8, 32, COLS), BF16),
            pltpu.VMEM((8, 32, COLS), BF16),
            pltpu.VMEM((NSEC, 32, HD), F32),
            pltpu.VMEM((NSEC, 32, HD), F32),
            pltpu.VMEM((TOKENS, RANK), F32),
            pltpu.VMEM((2, TOKENS, COLS), BF16),
            pltpu.VMEM((2, WIN, COLS), F32),
            pltpu.VMEM((6, COLS, COLS), BF16),
            pltpu.VMEM((6, COLS, COLS), BF16),
            dma((9,)), dma((12,)), dma((12,)), dma((10,)), dma((10,)), dma((3,)), dma((4,)),
            dma((15,)), dma((16,)), dma((15,)), dma((16,)),
            dma((15,)), dma((16,)),
            dma((2, PARTS, STEPS)), dma((2, PARTS, STEPS)),
            dma((PARTS,)), dma((PARTS,)), dma((6,)), dma((6,)),
            dma((4,)), dma((4,)), dma((4,)), dma((4,)), dma((8,)), dma((2,)), dma((15,)), dma((16,)),
        ],
        compiler_params=pltpu.CompilerParams(
            collective_id=0, has_side_effects=True, vmem_limit_bytes=VMEM_LIMIT
        ),
        name="attention_block_backward",
    )(ids, q, k, v, g, seg, upt, down, residual, hidden, embedding, weight)


def copy_kernel(*refs):
    count = len(refs) // 2
    sems = refs[-1]
    copies = [
        pltpu.make_async_copy(refs[n], refs[count + n], sems.at[n]) for n in range(count)
    ]
    for copy in copies:
        copy.start()
    for copy in copies:
        copy.wait()


def copy_call(arrays):
    anys = pl.BlockSpec(memory_space=pl.ANY)
    return pl.pallas_call(
        copy_kernel,
        out_shape=tuple(jax.ShapeDtypeStruct(a.shape, a.dtype) for a in arrays),
        in_specs=[anys] * len(arrays),
        out_specs=(anys,) * len(arrays),
        scratch_shapes=[pltpu.SemaphoreType.DMA((len(arrays),))],
        compiler_params=pltpu.CompilerParams(vmem_limit_bytes=VMEM_LIMIT),
        name="hand_over",
    )(*arrays)


def on_device(
    saved_queries,
    saved_keys,
    values,
    attention_output_grad,
    segments,
    hidden,
    embedding,
    section_block_index,
    shared_query_weight,
    adapter_down_factor,
    adapter_up_factor,
    residual,
):
    results = whole_call(
        section_block_index[:, 0],
        saved_queries[0].T,
        saved_keys[0].T,
        values[0].T,
        attention_output_grad[0].T,
        segments[None, :],
        adapter_up_factor[0].T,
        adapter_down_factor[0],
        residual[0],
        hidden[0],
        embedding,
        shared_query_weight,
    )
    kgt, vgt, down_grad, ugt, weight_grad, passed, embed_grad = copy_call(results)
    return (
        kgt.T[None],
        vgt.T[None],
        down_grad[None],
        ugt.T[None],
        weight_grad,
        passed[None],
        embed_grad,
    )


def solution(mesh):
    in_specs = (
        P("section", None, "tp"),
        P("section", None, "tp"),
        P("section", None, "tp"),
        P("section", None, "tp"),
        P(),
        P("section", None, None),
        P(),
        P(),
        P(None, "section", "tp"),
        P("section", "tp", None),
        P("section", None, "tp"),
        P("section", "tp", None),
    )
    out_specs = (
        P("section", None, "tp"),
        P("section", None, "tp"),
        P("section", "tp", None),
        P("section", None, "tp"),
        P(None, "section", "tp"),
        P("section", "tp", None),
        P("tp", "section"),
    )
    return jax.shard_map(
        on_device, mesh=mesh, in_specs=in_specs, out_specs=out_specs, check_vma=False
    )
```

```python
import jax
import jax.numpy as jnp
from jax import lax
from jax.experimental import pallas as pl
from jax.experimental.pallas import tpu as pltpu
from jax.sharding import PartitionSpec as P

MESH = pl.DeviceIdType.MESH
TOKENS = 512
WIDTH = 3584
COLS = 448
HD = 224
RANK = 128
WIN = 512
NSEC = 16
NTP = 16
SPLIT = 160
STEPS = 7
PARTS = 5
VMEM_LIMIT = 60 * 1024 * 1024
F32 = jnp.float32
BF16 = jnp.bfloat16


def dot_nt(a, b):
    return lax.dot_general(a, b, (((1,), (1,)), ((), ())), preferred_element_type=F32)


def dot_tn(a, b):
    return lax.dot_general(a, b, (((0,), (0,)), ((), ())), preferred_element_type=F32)


def dot_nn(a, b):
    return lax.dot_general(a, b, (((1,), (0,)), ((), ())), preferred_element_type=F32)


def remote(src, dst, send_sem, recv_sem, section, tp):
    return pltpu.make_async_remote_copy(
        src_ref=src,
        dst_ref=dst,
        send_sem=send_sem,
        recv_sem=recv_sem,
        device_id={"section": section, "tp": tp},
        device_id_type=MESH,
    )


def greet(peers):
    barrier = pltpu.get_barrier_semaphore()
    for section, tp in peers:
        pl.semaphore_signal(
            barrier, inc=1, device_id={"section": section, "tp": tp}, device_id_type=MESH
        )
    pl.semaphore_wait(barrier, len(peers))


def attention(q_ref, k_ref, v_ref, g_ref, seg_ref, qg, qgt, kg_ref, vg_ref):
    scale = HD ** (-0.5)
    seg_col = jnp.transpose(jnp.broadcast_to(seg_ref[...], (RANK, TOKENS)))[:, 0:1]
    key_id = lax.broadcasted_iota(jnp.int32, (TOKENS, TOKENS), 0)
    query_id = lax.broadcasted_iota(jnp.int32, (TOKENS, TOKENS), 1)
    allowed = (key_id <= query_id) & (seg_col == seg_ref[...])
    for head in range(2):
        rows = pl.ds(head * HD, HD)
        q, k, v, g = q_ref[rows, :], k_ref[rows, :], v_ref[rows, :], g_ref[rows, :]
        scores = jnp.where(allowed, dot_tn(k, q) * scale, -1e30)
        expo = jnp.exp(scores - jnp.max(scores, axis=0, keepdims=True))
        probs = expo / jnp.sum(expo, axis=0, keepdims=True)
        low = probs.astype(BF16)
        grad = dot_tn(v, g)
        delta = jnp.sum(low.astype(F32) * grad, axis=0, keepdims=True)
        dscore = (probs * (grad - delta)).astype(BF16)
        dq = (dot_nn(k, dscore) * scale).astype(BF16)
        qgt[rows, :] = dq
        qg[:, rows] = jnp.transpose(dq)
        kg_ref[rows, :] = (dot_nt(q, dscore) * scale).astype(BF16)
        vg_ref[rows, :] = dot_nt(g, low).astype(BF16)


def whole_kernel(
    ids, q_hbm, k_hbm, v_hbm, g_hbm, seg_ref, upt_ref, down_ref, res_ref, hidden, embedding, weight,
    kg_ref, vg_ref, dg_ref, ugt_ref, wsum_ref, passed_ref, embed_ref,
    qg, qgt, qg4, hid4, wg, embw, jw, adp, adw, bgrp, bpart, bland, bown, ball,
    heads, partial, ring, hland, total, etotal, pland, eland, nland, fbuf, qb, acc, dws, dwl,
    loc_sem, ws_sem, wr_sem, hs_sem, hr_sem, qs_sem, qr_sem, bs_sem, br_sem, cs_sem, cr_sem,
    gs_sem, gr_sem, rs_sem, rr_sem, is_sem, ir_sem, xs_sem, xr_sem,
    ps_sem, pr_sem, es_sem, er_sem, fin_sem, ns_sem,
):
    s = lax.axis_index("section")
    t = lax.axis_index("tp")
    y, j = s // 4, s % 4
    lo, c = j // 2, j % 2
    hi, z = t // 8, t % 8
    sib = y * 4 + 2 * lo + (1 - c)
    across = [y * 4 + 2 * (1 - lo) + i for i in range(2)]
    partner = y * 4 + 2 * (1 - lo) + c
    t_far = (1 - hi) * 8 + z
    yl, yr, yo = (y + 3) % 4, (y + 1) % 4, (y + 2) % 4
    left, right = yl * 4 + j, yr * 4 + j
    z_next, z_prev = hi * 8 + (z + 1) % 8, hi * 8 + (z + 7) % 8
    tp_peers = [(t + i) % NTP for i in range(1, NTP)]
    section_peers = [(s + i) % NSEC for i in range(1, NSEC)]
    loads = [
        pltpu.make_async_copy(array, heads.at[n], loc_sem.at[9 + n])
        for n, array in enumerate((q_hbm, k_hbm, v_hbm, g_hbm))
    ]
    for load in loads:
        load.start()
    greet(
        [(p, t) for p in section_peers]
        + [(s, p) for p in tp_peers]
        + [(a, t_far) for a in across]
    )
    sent = []

    def go(copy):
        copy.start()
        sent.append(copy)
        return copy

    def row_block(b, owner_y):
        return wg.at[b, pl.ds(pl.multiple_of(owner_y * COLS, 64), COLS), :]

    for n, (b, dest, slot) in enumerate([(0, right, 0), (1, left, 3), (1, right, 1), (0, left, 2)]):
        go(remote(weight.at[b], row_block(b, y), ws_sem.at[n], wr_sem.at[slot], dest, t))

    def w_on(n, b, owner_y, dest):
        return remote(row_block(b, owner_y), row_block(b, owner_y), ws_sem.at[n], wr_sem.at[n], dest, t)

    def w_wait(b, owner_y, slot):
        remote(weight.at[b], row_block(b, owner_y), ws_sem.at[0], wr_sem.at[slot], left, t).wait_recv()

    adder = t % 4
    half = (t // 4) % 2
    mine = pl.ds(pl.multiple_of(half * COLS, 64), COLS)
    rest = pl.ds(pl.multiple_of((1 - half) * COLS, 64), COLS)

    def down_copy(n):
        return remote(down_ref, adw.at[n, mine, :], gs_sem.at[0], gr_sem.at[n], y * 4 + adder, t)

    def back_copy(n):
        return remote(
            ball.at[:, :, pl.ds(0, RANK)], bgrp.at[n], gs_sem.at[1], gr_sem.at[4 + n], y * 4 + adder, t
        )

    adw[:, rest, :] = jnp.zeros((4, COLS, RANK), BF16)

    @pl.when(j != adder)
    def _():
        down_copy(j).start()

    @pl.when(j == adder)
    def _():
        adw[j, mine, :] = down_ref[...]

    def window(lo_d, c_d, part):
        return pl.ds(pl.multiple_of(896 * lo_d + 384 * c_d + 1792 * part, 128), WIN)

    def send_far(part):
        for i in range(2):
            go(remote(
                hidden.at[pl.ds(SPLIT, TOKENS - SPLIT), window(1 - lo, i, part)],
                hid4.at[j, part, pl.ds(SPLIT, TOKENS - SPLIT), :],
                hs_sem.at[5 * part + i], hr_sem.at[6 + 2 * c + part], across[i], t_far,
            ))

    def send_near(part):
        for i in range(2):
            go(remote(
                hidden.at[pl.ds(0, SPLIT), window(1 - lo, i, part)],
                hid4.at[j, part, pl.ds(0, SPLIT), :],
                hs_sem.at[5 * part + 2 + i], hr_sem.at[2 + 2 * c + part], across[i], t,
            ))
        go(remote(
            hidden.at[:, window(lo, 1 - c, part)], hid4.at[j, part],
            hs_sem.at[5 * part + 4], hr_sem.at[part], sib, t,
        ))

    locals_ = []

    def here(src, dst):
        copy = pltpu.make_async_copy(src, dst, loc_sem.at[len(locals_)])
        copy.start()
        locals_.append(copy)

    jwin = pl.ds(pl.multiple_of(896 * (z // 2) + 384 * (z % 2), 128), WIN)
    from_hidden = pltpu.make_async_copy(hidden.at[:, jwin], jw, loc_sem.at[8])
    from_embedding = pltpu.make_async_copy(embedding.at[:, jwin], jw, loc_sem.at[8])

    @pl.when(t < 8)
    def _():
        from_hidden.start()

    @pl.when(t >= 8)
    def _():
        from_embedding.start()

    send_far(0)
    for b in range(2):
        here(weight.at[b], row_block(b, y))
    for part in range(2):
        here(hidden.at[:, window(lo, c, part)], hid4.at[j, part])
        here(embedding.at[:, window(lo, c, part)], embw.at[part])

    n_copy = remote(res_ref, nland, ns_sem.at[0], ns_sem.at[1], (s + NSEC - 1) % NSEC, t)

    for load in loads:
        load.wait()
    attention(
        heads.at[0], heads.at[1], heads.at[2], heads.at[3], seg_ref, qg, qgt, kg_ref, vg_ref
    )

    go(remote(qg, qg4.at[j], qs_sem.at[0], qr_sem.at[j], partner, t))
    go(remote(qg, qg4.at[j], qs_sem.at[1], qr_sem.at[j], sib, t))
    qg4[j] = qg[...]

    adp[...] = jnp.zeros_like(adp)
    adp[pl.ds(pl.multiple_of(64 * (z % 2), 64), COLS), :] = down_ref[...]
    bpart[:, :, 0:RANK] = dot_nn(qg[...], upt_ref[...]).reshape(NTP, 32, RANK).astype(BF16)
    from_hidden.wait()
    bpart[:, :, RANK : 2 * RANK] = dot_nn(jw[...], adp[...]).reshape(NTP, 32, RANK).astype(BF16)
    for n, peer in enumerate(tp_peers):
        go(remote(bpart.at[peer], bland.at[t], bs_sem.at[n], br_sem.at[t], s, peer))
    bland[t] = bpart[t]
    send_near(0)

    w_wait(0, yl, 0)
    go(w_on(4, 0, yl, right))
    w_wait(1, yr, 3)
    go(w_on(5, 1, yr, left))

    for peer in tp_peers:
        remote(bpart.at[peer], bland.at[peer], bs_sem.at[0], br_sem.at[peer], s, peer).wait_recv()
    bown[...] = jnp.sum(bland[...].astype(F32), axis=0).astype(BF16)
    for n, peer in enumerate(tp_peers):
        go(remote(bown, ball.at[t], cs_sem.at[n], cr_sem.at[t], s, peer))
    ball[t] = bown[...]

    def wait_q(slot):
        remote(qg, qg4.at[slot], qs_sem.at[0], qr_sem.at[slot], sib, t).wait_recv()

    slot_partner = 2 * (1 - lo) + c
    wait_q(slot_partner)
    go(remote(
        qg4.at[slot_partner], qg4.at[slot_partner], qs_sem.at[2], qr_sem.at[slot_partner], sib, t
    ))

    for peer in tp_peers:
        remote(bown, ball.at[peer], cs_sem.at[0], cr_sem.at[peer], s, peer).wait_recv()

    @pl.when(j != adder)
    def _():
        back_copy(j).start()

    @pl.when(j == adder)
    def _():
        bgrp[j] = ball[:, :, 0:RANK]

    send_far(1)
    send_near(1)
    go(n_copy)
    wait_q(2 * lo + 1 - c)
    wait_q(2 * (1 - lo) + 1 - c)

    def keep(n, b):
        return jnp.where(ids[4 * y + n] == b, 1.0, 0.0).astype(F32)

    for b in range(2):
        picked = qg4[0].astype(F32) * keep(0, b)
        for n in range(1, 4):
            picked = picked + qg4[n].astype(F32) * keep(n, b)
        qb[b] = picked.astype(BF16)
    for copy in locals_:
        copy.wait()

    @pl.when(j == adder)
    def _():
        for n in range(4):
            @pl.when(j != n)
            def _():
                down_copy(n).wait_recv()
                back_copy(n).wait_recv()

    w_wait(1, yl, 1)
    w_wait(0, yr, 2)
    w_wait(0, yo, 4)
    w_wait(1, yo, 5)

    def chunk(d, k):
        return (z + 15 - k) % 8 if d == 0 else 8 + (z + 1 + k) % 8

    def hop(d, p, k):
        return remote(
            partial.at[chunk(d, k), p], ring.at[d, p, k],
            rs_sem.at[d, p, k], rr_sem.at[d, p, k], s, z_next if d == 0 else z_prev,
        )

    def store(p):
        partial[:, p] = fbuf[...].reshape(NTP, 32, 2 * COLS).astype(BF16)
        for d in range(2):
            go(hop(d, p, 0))

    def advance(p, k):
        for d in range(2):
            hop(d, p, k - 1).wait_recv()
            partial[chunk(d, k), p] = (
                partial[chunk(d, k), p].astype(F32) + ring[d, p, k - 1].astype(F32)
            ).astype(BF16)
            if k < STEPS:
                go(hop(d, p, k))

    for p in range(4):
        picked = wg[0, 0 : 2 * COLS, :] * keep(p, 0).astype(BF16) + wg[
            1, 0 : 2 * COLS, :
        ] * keep(p, 1).astype(BF16)
        fbuf[...] = dot_nt(qg4[p], picked)

        @pl.when((j == adder) & (t < 8))
        def _():
            fbuf[...] += dot_nt(bgrp[p].reshape(TOKENS, RANK), adw[p])

        store(p)
    fbuf[...] = dot_nt(qb[0], wg[0, 2 * COLS :, :]) + dot_nt(qb[1], wg[1, 2 * COLS :, :])

    @pl.when((j == adder) & (t >= 8))
    def _():
        for n in range(4):
            fbuf[...] += dot_nt(bgrp[n].reshape(TOKENS, RANK), adw[n])

    store(4)

    def wait_hidden():
        for part in range(2):
            remote(
                hidden.at[:, window(lo, c, part)], hid4.at[2 * lo + 1 - c, part],
                hs_sem.at[0], hr_sem.at[part], sib, t,
            ).wait_recv()
            for i in range(2):
                for first, count, base in ((0, SPLIT, 2), (SPLIT, TOKENS - SPLIT, 6)):
                    remote(
                        hidden.at[pl.ds(first, count), window(lo, c, part)],
                        hid4.at[2 * (1 - lo) + i, part, pl.ds(first, count), :],
                        hs_sem.at[0], hr_sem.at[base + 2 * i + part], sib, t,
                    ).wait_recv()

    skip = pl.ds(pl.multiple_of(64 * c, 64), COLS)

    def weight_rows(yd):
        @pl.when(yd < 2)
        def _():
            for n in range(4):
                term = dot_tn(hid4[n, yd % 2], qg4[n])
                for b in range(2):
                    if n == 0:
                        acc[b] = term * keep(n, b)
                    else:
                        acc[b] += term * keep(n, b)

        @pl.when(yd >= 2)
        def _():
            for b in range(2):
                acc[b] = dot_tn(embw[yd % 2], qb[b])

    def x_copy(n):
        to_right = n in (0, 2, 3)
        return remote(dws.at[n], dwl.at[n], xs_sem.at[n], xr_sem.at[n], right if to_right else left, t)

    def weight_far():
        weight_rows(yo)
        for b in range(2):
            dws[b] = acc[b, skip, :].astype(BF16)
            go(x_copy(b))

    def weight_near(side):
        weight_rows((yr, yl)[side])
        base = 2 + 2 * side
        for b in (1 - side, side):
            dws[base + b] = acc[b, skip, :].astype(BF16)
        go(x_copy(base + 1 - side))

    def weight_on(side):
        x_copy(side).wait_recv()
        n = 2 + 3 * side
        dws[n] = (dws[n].astype(F32) + dwl[side].astype(F32)).astype(BF16)
        go(x_copy(n))

    def weight_own():
        weight_rows(y)

    for k in range(1, STEPS):
        for p in range(PARTS):
            advance(p, k)
        if k == 1:
            ugt_ref[...] = dot_nn(qgt[...], ball[:, :, RANK : 2 * RANK].reshape(TOKENS, RANK))
            fbuf[:, 0:RANK] = dot_tn(jw[...], ball[:, :, 0:RANK].reshape(TOKENS, RANK))
            dg_ref[...] = fbuf[pl.ds(pl.multiple_of(64 * (z % 2), 64), COLS), 0:RANK]
        if k == 2:
            wait_hidden()
            weight_far()
        if k == 3:
            weight_near(0)
            weight_near(1)
        if k == 4:
            weight_on(0)
            weight_on(1)
        if k == 5:
            weight_own()

    def swap(p):
        return remote(
            partial.at[(1 - hi) * 8 + z, p], hland.at[p], is_sem.at[p], ir_sem.at[p], s, t_far
        )

    def move(src, dst, send_sem, recv_sem, here_sem, dest):
        away = remote(src, dst, send_sem, recv_sem, dest, t)
        near = pltpu.make_async_copy(src, dst, here_sem)

        @pl.when(dest != s)
        def _():
            away.start()

        @pl.when(dest == s)
        def _():
            near.start()

        def finish():
            @pl.when(dest != s)
            def _():
                away.wait_send()

            @pl.when(dest == s)
            def _():
                near.wait()

        return finish

    ends = []

    def joined_halves(p):
        swap(p).wait_recv()
        return partial[hi * 8 + z, p].astype(F32) + hland[p].astype(F32)

    for p in range(PARTS):
        advance(p, STEPS)
        go(swap(p))
    for n in (2, 3, 4, 5):
        x_copy(n).wait_recv()
    for b in range(2):
        wsum_ref[b] = acc[b, skip, :] + (dwl[2 + b].astype(F32) + dwl[4 + b].astype(F32))
    for p in range(4):
        total[p] = joined_halves(p).astype(BF16)
        dest = (y * 4 + p + NSEC - 1) % NSEC
        ends.append(move(total.at[p], pland.at[j], ps_sem.at[p], pr_sem.at[j], fin_sem.at[p], dest))
    value = joined_halves(4)
    for n in range(4):
        etotal[n] = value[:, n * HD : (n + 1) * HD]
        dest = 2 * j + n % 2 + 8 * (n // 2)
        ends.append(
            move(etotal.at[n], eland.at[y], es_sem.at[n], er_sem.at[y], fin_sem.at[4 + n], dest)
        )
    n_copy.wait_recv()
    for n in range(4):
        source = (((s + 1) % NSEC) // 4) * 4 + n

        @pl.when(source != s)
        def _():
            remote(total.at[n], pland.at[n], ps_sem.at[n], pr_sem.at[n], source, t).wait_recv()

    for end in ends:
        end()
    more = jnp.where(s == NSEC - 1, 0.0, 1.0).astype(F32)
    for n in range(8):
        half = pland[n % 4].astype(F32)[:, (n // 4) * COLS : (n // 4 + 1) * COLS]
        passed_ref[:, n * COLS : (n + 1) * COLS] = (
            (nland[:, n * COLS : (n + 1) * COLS].astype(F32) + half) * more
        ).astype(BF16)
    for n in range(4):
        source = n * 4 + (s % 8) // 2

        @pl.when(source != s)
        def _():
            remote(etotal.at[n], eland.at[n], es_sem.at[n], er_sem.at[n], source, t).wait_recv()

    embed_ref[...] = jnp.sum(eland[...], axis=0)
    for copy in sent:
        copy.wait_send()

    @pl.when(j != adder)
    def _():
        down_copy(j).wait_send()
        back_copy(j).wait_send()


def whole_call(ids, q, k, v, g, seg, upt, down, residual, hidden, embedding, weight):
    vm = pl.BlockSpec(memory_space=pltpu.VMEM)
    sm = pl.BlockSpec(memory_space=pltpu.SMEM)
    anys = pl.BlockSpec(memory_space=pl.ANY)
    dma = pltpu.SemaphoreType.DMA
    out = jax.ShapeDtypeStruct
    return pl.pallas_call(
        whole_kernel,
        out_shape=(
            out((COLS, TOKENS), BF16),
            out((COLS, TOKENS), BF16),
            out((COLS, RANK), F32),
            out((COLS, RANK), F32),
            out((2, COLS, COLS), F32),
            out((32, WIDTH), BF16),
            out((32, HD), F32),
        ),
        in_specs=[sm] + [anys] * 4 + [vm] * 3 + [anys] * 4,
        out_specs=(vm,) * 7,
        scratch_shapes=[
            pltpu.VMEM((TOKENS, COLS), BF16),
            pltpu.VMEM((COLS, TOKENS), BF16),
            pltpu.VMEM((4, TOKENS, COLS), BF16),
            pltpu.VMEM((4, 2, TOKENS, WIN), BF16),
            pltpu.VMEM((2, 4 * COLS, COLS), BF16),
            pltpu.VMEM((2, TOKENS, WIN), BF16),
            pltpu.VMEM((TOKENS, WIN), BF16),
            pltpu.VMEM((WIN, RANK), BF16),
            pltpu.VMEM((4, 2 * COLS, RANK), BF16),
            pltpu.VMEM((4, NTP, 32, RANK), BF16),
            pltpu.VMEM((NTP, 32, 2 * RANK), BF16),
            pltpu.VMEM((NTP, 32, 2 * RANK), BF16),
            pltpu.VMEM((32, 2 * RANK), BF16),
            pltpu.VMEM((NTP, 32, 2 * RANK), BF16),
            pltpu.VMEM((4, COLS, TOKENS), BF16),
            pltpu.VMEM((NTP, PARTS, 32, 2 * COLS), BF16),
            pltpu.VMEM((2, PARTS, STEPS, 32, 2 * COLS), BF16),
            pltpu.VMEM((PARTS, 32, 2 * COLS), BF16),
            pltpu.VMEM((4, 32, 2 * COLS), BF16),
            pltpu.VMEM((4, 32, HD), F32),
            pltpu.VMEM((4, 32, 2 * COLS), BF16),
            pltpu.VMEM((4, 32, HD), F32),
            pltpu.VMEM((32, WIDTH), BF16),
            pltpu.VMEM((TOKENS, 2 * COLS), F32),
            pltpu.VMEM((2, TOKENS, COLS), BF16),
            pltpu.VMEM((2, WIN, COLS), F32),
            pltpu.VMEM((6, COLS, COLS), BF16),
            pltpu.VMEM((6, COLS, COLS), BF16),
            dma((13,)), dma((6,)), dma((6,)), dma((10,)), dma((10,)), dma((3,)), dma((4,)),
            dma((15,)), dma((16,)), dma((15,)), dma((16,)),
            dma((2,)), dma((8,)),
            dma((2, PARTS, STEPS)), dma((2, PARTS, STEPS)),
            dma((PARTS,)), dma((PARTS,)), dma((6,)), dma((6,)),
            dma((4,)), dma((4,)), dma((4,)), dma((4,)), dma((8,)), dma((2,)),
        ],
        compiler_params=pltpu.CompilerParams(
            collective_id=0, has_side_effects=True, vmem_limit_bytes=VMEM_LIMIT
        ),
        name="attention_block_backward",
    )(ids, q, k, v, g, seg, upt, down, residual, hidden, embedding, weight)


def copy_kernel(*refs):
    count = (len(refs) - 1) // 3
    sems = refs[-1]
    ins, outs, held = refs[:count], refs[count : 2 * count], refs[2 * count : 3 * count]
    coming = [pltpu.make_async_copy(ins[n], held[n], sems.at[0, n]) for n in range(count)]
    going = [pltpu.make_async_copy(held[n], outs[n], sems.at[1, n]) for n in range(count)]
    for copy in coming:
        copy.start()
    for n in range(count):
        coming[n].wait()
        going[n].start()
    for copy in going:
        copy.wait()


def copy_call(arrays):
    anys = pl.BlockSpec(memory_space=pl.ANY)
    return pl.pallas_call(
        copy_kernel,
        out_shape=tuple(jax.ShapeDtypeStruct(a.shape, a.dtype) for a in arrays),
        in_specs=[anys] * len(arrays),
        out_specs=(anys,) * len(arrays),
        scratch_shapes=[pltpu.VMEM(a.shape, a.dtype) for a in arrays]
        + [pltpu.SemaphoreType.DMA((2, len(arrays)))],
        compiler_params=pltpu.CompilerParams(vmem_limit_bytes=VMEM_LIMIT),
        name="hand_over",
    )(*arrays)


def on_device(
    saved_queries,
    saved_keys,
    values,
    attention_output_grad,
    segments,
    hidden,
    embedding,
    section_block_index,
    shared_query_weight,
    adapter_down_factor,
    adapter_up_factor,
    residual,
):
    results = whole_call(
        section_block_index[:, 0],
        saved_queries[0].T,
        saved_keys[0].T,
        values[0].T,
        attention_output_grad[0].T,
        segments[None, :],
        adapter_up_factor[0].T,
        adapter_down_factor[0],
        residual[0],
        hidden[0],
        embedding,
        shared_query_weight,
    )
    kgt, vgt, down_grad, ugt, weight_grad, passed, embed_grad = copy_call(results)
    return (
        kgt.T[None],
        vgt.T[None],
        down_grad[None],
        ugt.T[None],
        weight_grad,
        passed[None],
        embed_grad,
    )


def solution(mesh):
    in_specs = (
        P("section", None, "tp"),
        P("section", None, "tp"),
        P("section", None, "tp"),
        P("section", None, "tp"),
        P(),
        P("section", None, None),
        P(),
        P(),
        P(None, "section", "tp"),
        P("section", "tp", None),
        P("section", None, "tp"),
        P("section", "tp", None),
    )
    out_specs = (
        P("section", None, "tp"),
        P("section", None, "tp"),
        P("section", "tp", None),
        P("section", None, "tp"),
        P(None, "section", "tp"),
        P("section", "tp", None),
        P("tp", "section"),
    )
    return jax.shard_map(
        on_device, mesh=mesh, in_specs=in_specs, out_specs=out_specs, check_vma=False
    )
```

```python
import jax
import jax.numpy as jnp
from jax import lax
from jax.experimental import pallas as pl
from jax.experimental.pallas import tpu as pltpu
from jax.sharding import PartitionSpec as P

MESH = pl.DeviceIdType.MESH
TOKENS = 512
WIDTH = 3584
COLS = 448
HD = 224
RANK = 128
WIN = 512
NSEC = 16
NTP = 16
SPLIT = 160
STEPS = 7
PARTS = 4
VMEM_LIMIT = 60 * 1024 * 1024
F32 = jnp.float32
BF16 = jnp.bfloat16


def dot_nt(a, b):
    return lax.dot_general(a, b, (((1,), (1,)), ((), ())), preferred_element_type=F32)


def dot_tn(a, b):
    return lax.dot_general(a, b, (((0,), (0,)), ((), ())), preferred_element_type=F32)


def dot_nn(a, b):
    return lax.dot_general(a, b, (((1,), (0,)), ((), ())), preferred_element_type=F32)


def remote(src, dst, send_sem, recv_sem, section, tp):
    return pltpu.make_async_remote_copy(
        src_ref=src,
        dst_ref=dst,
        send_sem=send_sem,
        recv_sem=recv_sem,
        device_id={"section": section, "tp": tp},
        device_id_type=MESH,
    )


def greet(peers):
    barrier = pltpu.get_barrier_semaphore()
    for section, tp in peers:
        pl.semaphore_signal(
            barrier, inc=1, device_id={"section": section, "tp": tp}, device_id_type=MESH
        )
    pl.semaphore_wait(barrier, len(peers))


def attention(q_ref, k_ref, v_ref, g_ref, seg_ref, qg, qgt, kg_ref, vg_ref):
    scale = HD ** (-0.5)
    seg_col = jnp.transpose(jnp.broadcast_to(seg_ref[...], (RANK, TOKENS)))[:, 0:1]
    key_id = lax.broadcasted_iota(jnp.int32, (TOKENS, TOKENS), 0)
    query_id = lax.broadcasted_iota(jnp.int32, (TOKENS, TOKENS), 1)
    allowed = (key_id <= query_id) & (seg_col == seg_ref[...])
    for head in range(2):
        rows = pl.ds(head * HD, HD)
        q, k, v, g = q_ref[rows, :], k_ref[rows, :], v_ref[rows, :], g_ref[rows, :]
        scores = jnp.where(allowed, dot_tn(k, q) * scale, -1e30)
        expo = jnp.exp(scores - jnp.max(scores, axis=0, keepdims=True))
        probs = expo / jnp.sum(expo, axis=0, keepdims=True)
        low = probs.astype(BF16)
        grad = dot_tn(v, g)
        delta = jnp.sum(low.astype(F32) * grad, axis=0, keepdims=True)
        dscore = (probs * (grad - delta)).astype(BF16)
        dq = (dot_nn(k, dscore) * scale).astype(BF16)
        qgt[rows, :] = dq
        qg[:, rows] = jnp.transpose(dq)
        kg_ref[rows, :] = (dot_nt(q, dscore) * scale).astype(BF16)
        vg_ref[rows, :] = dot_nt(g, low).astype(BF16)


def whole_kernel(
    ids, q_hbm, k_hbm, v_hbm, g_hbm, seg_ref, upt_ref, down_ref, res_ref, hidden, embedding, weight,
    kg_ref, vg_ref, dg_ref, ugt_ref, wsum_ref, passed_ref, embed_ref,
    qg, qgt, qg4, hid4, wg, embw, jw, adp, adw, bgrp, bpart, bland, bown, ball,
    heads, partial, ring, pland, nland, ebuf, eyl, epart, ering, efin, fbuf, qb, acc, dws, dwl,
    loc_sem, ws_sem, wr_sem, hs_sem, hr_sem, qs_sem, qr_sem, bs_sem, br_sem, cs_sem, cr_sem,
    gs_sem, gr_sem, rs_sem, rr_sem, xs_sem, xr_sem,
    ps_sem, pr_sem, es_sem, er_sem, fin_sem, ns_sem, ys_sem, yr_sem, us_sem, ur_sem,
):
    s = lax.axis_index("section")
    t = lax.axis_index("tp")
    y, j = s // 4, s % 4
    lo, c = j // 2, j % 2
    hi, z = t // 8, t % 8
    sib = y * 4 + 2 * lo + (1 - c)
    across = [y * 4 + 2 * (1 - lo) + i for i in range(2)]
    partner = y * 4 + 2 * (1 - lo) + c
    t_far = (1 - hi) * 8 + z
    yl, yr, yo = (y + 3) % 4, (y + 1) % 4, (y + 2) % 4
    left, right = yl * 4 + j, yr * 4 + j
    z_next, z_prev = hi * 8 + (z + 1) % 8, hi * 8 + (z + 7) % 8
    tp_peers = [(t + i) % NTP for i in range(1, NTP)]
    section_peers = [(s + i) % NSEC for i in range(1, NSEC)]
    loads = [
        pltpu.make_async_copy(array, heads.at[n], loc_sem.at[9 + n])
        for n, array in enumerate((q_hbm, k_hbm, v_hbm, g_hbm))
    ]
    for load in loads:
        load.start()
    greet(
        [(p, t) for p in section_peers]
        + [(s, p) for p in tp_peers]
        + [(p, t_far) for p in section_peers]
    )
    sent = []

    def go(copy):
        copy.start()
        sent.append(copy)
        return copy

    def row_block(b, owner_y):
        return wg.at[b, pl.ds(pl.multiple_of(owner_y * COLS, 64), COLS), :]

    for n, (b, dest, slot) in enumerate([(0, right, 0), (1, left, 3), (1, right, 1), (0, left, 2)]):
        go(remote(weight.at[b], row_block(b, y), ws_sem.at[n], wr_sem.at[slot], dest, t))

    def w_on(n, b, owner_y, dest):
        return remote(row_block(b, owner_y), row_block(b, owner_y), ws_sem.at[n], wr_sem.at[n], dest, t)

    def w_wait(b, owner_y, slot):
        remote(weight.at[b], row_block(b, owner_y), ws_sem.at[0], wr_sem.at[slot], left, t).wait_recv()

    adder = t % 4
    half = (t // 4) % 2
    mine = pl.ds(pl.multiple_of(half * COLS, 64), COLS)
    rest = pl.ds(pl.multiple_of((1 - half) * COLS, 64), COLS)

    def down_copy(n):
        return remote(down_ref, adw.at[n, mine, :], gs_sem.at[0], gr_sem.at[n], y * 4 + adder, t)

    def back_copy(n):
        return remote(
            ball.at[:, :, pl.ds(0, RANK)], bgrp.at[n], gs_sem.at[1], gr_sem.at[4 + n], y * 4 + adder, t
        )

    adw[:, rest, :] = jnp.zeros((4, COLS, RANK), BF16)

    @pl.when(j != adder)
    def _():
        down_copy(j).start()

    @pl.when(j == adder)
    def _():
        adw[j, mine, :] = down_ref[...]

    def window(lo_d, c_d, part):
        return pl.ds(pl.multiple_of(896 * lo_d + 384 * c_d + 1792 * part, 128), WIN)

    def send_far(part):
        for i in range(2):
            go(remote(
                hidden.at[pl.ds(SPLIT, TOKENS - SPLIT), window(1 - lo, i, part)],
                hid4.at[j, part, pl.ds(SPLIT, TOKENS - SPLIT), :],
                hs_sem.at[5 * part + i], hr_sem.at[6 + 2 * c + part], across[i], t_far,
            ))

    def send_near(part):
        for i in range(2):
            go(remote(
                hidden.at[pl.ds(0, SPLIT), window(1 - lo, i, part)],
                hid4.at[j, part, pl.ds(0, SPLIT), :],
                hs_sem.at[5 * part + 2 + i], hr_sem.at[2 + 2 * c + part], across[i], t,
            ))
        go(remote(
            hidden.at[:, window(lo, 1 - c, part)], hid4.at[j, part],
            hs_sem.at[5 * part + 4], hr_sem.at[part], sib, t,
        ))

    locals_ = []

    def here(src, dst):
        copy = pltpu.make_async_copy(src, dst, loc_sem.at[len(locals_)])
        copy.start()
        locals_.append(copy)

    jwin = pl.ds(pl.multiple_of(896 * (z // 2) + 384 * (z % 2), 128), WIN)
    from_hidden = pltpu.make_async_copy(hidden.at[:, jwin], jw, loc_sem.at[8])
    from_embedding = pltpu.make_async_copy(embedding.at[:, jwin], jw, loc_sem.at[8])

    @pl.when(t < 8)
    def _():
        from_hidden.start()

    @pl.when(t >= 8)
    def _():
        from_embedding.start()

    send_far(0)
    for b in range(2):
        here(weight.at[b], row_block(b, y))
    for part in range(2):
        here(hidden.at[:, window(lo, c, part)], hid4.at[j, part])
        here(embedding.at[:, window(lo, c, part)], embw.at[part])

    n_copy = remote(res_ref, nland, ns_sem.at[0], ns_sem.at[1], (s + NSEC - 1) % NSEC, t)

    for load in loads:
        load.wait()
    attention(
        heads.at[0], heads.at[1], heads.at[2], heads.at[3], seg_ref, qg, qgt, kg_ref, vg_ref
    )

    go(remote(qg, qg4.at[j], qs_sem.at[0], qr_sem.at[j], partner, t))
    go(remote(qg, qg4.at[j], qs_sem.at[1], qr_sem.at[j], sib, t))
    qg4[j] = qg[...]

    adp[...] = jnp.zeros_like(adp)
    adp[pl.ds(pl.multiple_of(64 * (z % 2), 64), COLS), :] = down_ref[...]
    bpart[:, :, 0:RANK] = dot_nn(qg[...], upt_ref[...]).reshape(NTP, 32, RANK).astype(BF16)
    from_hidden.wait()
    bpart[:, :, RANK : 2 * RANK] = dot_nn(jw[...], adp[...]).reshape(NTP, 32, RANK).astype(BF16)
    for n, peer in enumerate(tp_peers):
        go(remote(bpart.at[peer], bland.at[t], bs_sem.at[n], br_sem.at[t], s, peer))
    bland[t] = bpart[t]
    send_near(0)

    w_wait(0, yl, 0)
    go(w_on(4, 0, yl, right))
    w_wait(1, yr, 3)
    go(w_on(5, 1, yr, left))

    for peer in tp_peers:
        remote(bpart.at[peer], bland.at[peer], bs_sem.at[0], br_sem.at[peer], s, peer).wait_recv()
    bown[...] = jnp.sum(bland[...].astype(F32), axis=0).astype(BF16)
    for n, peer in enumerate(tp_peers):
        go(remote(bown, ball.at[t], cs_sem.at[n], cr_sem.at[t], s, peer))
    ball[t] = bown[...]

    def wait_q(slot):
        remote(qg, qg4.at[slot], qs_sem.at[0], qr_sem.at[slot], sib, t).wait_recv()

    slot_partner = 2 * (1 - lo) + c
    wait_q(slot_partner)
    go(remote(
        qg4.at[slot_partner], qg4.at[slot_partner], qs_sem.at[2], qr_sem.at[slot_partner], sib, t
    ))

    for peer in tp_peers:
        remote(bown, ball.at[peer], cs_sem.at[0], cr_sem.at[peer], s, peer).wait_recv()

    @pl.when(j != adder)
    def _():
        back_copy(j).start()

    @pl.when(j == adder)
    def _():
        bgrp[j] = ball[:, :, 0:RANK]

    send_far(1)
    send_near(1)
    go(n_copy)
    wait_q(2 * lo + 1 - c)
    wait_q(2 * (1 - lo) + 1 - c)

    def keep(n, b):
        return jnp.where(ids[4 * y + n] == b, 1.0, 0.0).astype(F32)

    for b in range(2):
        picked = qg4[0].astype(F32) * keep(0, b)
        for n in range(1, 4):
            picked = picked + qg4[n].astype(F32) * keep(n, b)
        qb[b] = picked.astype(BF16)
    for copy in locals_:
        copy.wait()

    @pl.when(j == adder)
    def _():
        for n in range(4):
            @pl.when(j != n)
            def _():
                down_copy(n).wait_recv()
                back_copy(n).wait_recv()

    w_wait(1, yl, 1)
    w_wait(0, yr, 2)
    w_wait(0, yo, 4)
    w_wait(1, yo, 5)

    def chunk(d, k):
        return (z + 15 - k) % 8 if d == 0 else 8 + (z + 1 + k) % 8

    def hop(d, p, k):
        return remote(
            partial.at[chunk(d, k), p], ring.at[d, p, k],
            rs_sem.at[d, p, k], rr_sem.at[d, p, k], s, z_next if d == 0 else z_prev,
        )

    def store(p):
        partial[:, p] = fbuf[...].reshape(NTP, 32, 2 * COLS).astype(BF16)
        for d in range(2):
            go(hop(d, p, 0))

    def advance(p, k):
        for d in range(2):
            hop(d, p, k - 1).wait_recv()
            partial[chunk(d, k), p] = (
                partial[chunk(d, k), p].astype(F32) + ring[d, p, k - 1].astype(F32)
            ).astype(BF16)
            if k < STEPS:
                go(hop(d, p, k))

    for n in range(4):
        cols = pl.ds(2 * COLS + n * HD, HD)
        fbuf[:, 0:HD] = dot_nt(qb[0], wg[0, cols, :]) + dot_nt(qb[1], wg[1, cols, :])

        @pl.when((j == adder) & (t >= 8))
        def _():
            for m in range(4):
                fbuf[:, 0:HD] += dot_nt(
                    bgrp[m].reshape(TOKENS, RANK), adw[m, n * HD : (n + 1) * HD, :]
                )

        ebuf[n] = fbuf[:, 0:HD].astype(BF16)

    def e_copy(i):
        yd = (y + i) % 4
        return remote(ebuf.at[yd], eyl.at[y], ys_sem.at[i - 1], yr_sem.at[y], yd * 4 + j, t)

    for i in (1, 3, 2):
        go(e_copy(i))

    def e_hop(d, k):
        return remote(
            epart.at[chunk(d, k)], ering.at[d, k], us_sem.at[d, k], ur_sem.at[d, k],
            s, z_next if d == 0 else z_prev,
        )

    def e_start():
        value = ebuf[y].astype(F32)
        for i in (1, 3, 2):
            ys = (y + i) % 4
            remote(ebuf.at[ys], eyl.at[ys], ys_sem.at[0], yr_sem.at[ys], s, t).wait_recv()
            value = value + eyl[ys].astype(F32)
        epart[...] = value.reshape(NTP, 32, HD).astype(BF16)
        for d in range(2):
            go(e_hop(d, 0))

    def e_advance(k):
        for d in range(2):
            e_hop(d, k - 1).wait_recv()
            epart[chunk(d, k)] = (
                epart[chunk(d, k)].astype(F32) + ering[d, k - 1].astype(F32)
            ).astype(BF16)
            if k < STEPS:
                go(e_hop(d, k))

    for p in range(4):
        picked = wg[0, 0 : 2 * COLS, :] * keep(p, 0).astype(BF16) + wg[
            1, 0 : 2 * COLS, :
        ] * keep(p, 1).astype(BF16)
        fbuf[...] = dot_nt(qg4[p], picked)

        @pl.when((j == adder) & (t < 8))
        def _():
            fbuf[...] += dot_nt(bgrp[p].reshape(TOKENS, RANK), adw[p])

        store(p)

    def wait_hidden():
        for part in range(2):
            remote(
                hidden.at[:, window(lo, c, part)], hid4.at[2 * lo + 1 - c, part],
                hs_sem.at[0], hr_sem.at[part], sib, t,
            ).wait_recv()
            for i in range(2):
                for first, count, base in ((0, SPLIT, 2), (SPLIT, TOKENS - SPLIT, 6)):
                    remote(
                        hidden.at[pl.ds(first, count), window(lo, c, part)],
                        hid4.at[2 * (1 - lo) + i, part, pl.ds(first, count), :],
                        hs_sem.at[0], hr_sem.at[base + 2 * i + part], sib, t,
                    ).wait_recv()

    skip = pl.ds(pl.multiple_of(64 * c, 64), COLS)

    def weight_rows(yd):
        @pl.when(yd < 2)
        def _():
            for n in range(4):
                term = dot_tn(hid4[n, yd % 2], qg4[n])
                for b in range(2):
                    if n == 0:
                        acc[b] = term * keep(n, b)
                    else:
                        acc[b] += term * keep(n, b)

        @pl.when(yd >= 2)
        def _():
            for b in range(2):
                acc[b] = dot_tn(embw[yd % 2], qb[b])

    def x_copy(n):
        to_right = n in (0, 2, 3)
        return remote(dws.at[n], dwl.at[n], xs_sem.at[n], xr_sem.at[n], right if to_right else left, t)

    upper = pl.ds(pl.multiple_of(64 * c, 32), HD)
    lower = pl.ds(pl.multiple_of(64 * c + HD, 32), HD)

    def stack(n, b):
        for i in range(3):
            dws[n, i * COLS : (i + 1) * COLS, :] = acc[
                b, skip, i * RANK : (i + 1) * RANK
            ].astype(BF16)
        ends_ = jnp.concatenate([acc[b, upper, 3 * RANK : COLS], acc[b, lower, 3 * RANK : COLS]], axis=1)
        dws[n, 3 * COLS : 3 * COLS + HD, :] = ends_.astype(BF16)

    def weight_far():
        weight_rows(yo)
        for b in range(2):
            stack(b, b)
            go(x_copy(b))

    def weight_near(side):
        weight_rows((yr, yl)[side])
        base = 2 + 2 * side
        for b in (1 - side, side):
            stack(base + b, b)
        go(x_copy(base + 1 - side))

    def weight_on(side):
        x_copy(side).wait_recv()
        n = 2 + 3 * side
        dws[n] = (dws[n].astype(F32) + dwl[side].astype(F32)).astype(BF16)
        go(x_copy(n))

    def weight_own():
        weight_rows(y)

    for k in range(1, STEPS):
        for p in range(PARTS):
            advance(p, k)
            if p == 1 and k == 2:
                e_start()
            if p == 1 and k > 2:
                e_advance(k - 2)
        if k == 1:
            ugt_ref[...] = dot_nn(qgt[...], ball[:, :, RANK : 2 * RANK].reshape(TOKENS, RANK))
            fbuf[:, 0:RANK] = dot_tn(jw[...], ball[:, :, 0:RANK].reshape(TOKENS, RANK))
            dg_ref[...] = fbuf[pl.ds(pl.multiple_of(64 * (z % 2), 64), COLS), 0:RANK]
        if k == 2:
            wait_hidden()
            weight_far()
        if k == 3:
            weight_near(0)
            weight_near(1)
        if k == 4:
            weight_on(0)
            weight_on(1)
        if k == 5:
            weight_own()
        if k == 6:
            e_advance(5)

    ends = []

    def move(src, dst, send_sem, recv_sem, here_sem, section, tp):
        away = remote(src, dst, send_sem, recv_sem, section, tp)
        near = pltpu.make_async_copy(src, dst, here_sem)
        stays = (section == s) & (tp == t)

        @pl.when(jnp.logical_not(stays))
        def _():
            away.start()

        @pl.when(stays)
        def _():
            near.start()

        def finish():
            @pl.when(jnp.logical_not(stays))
            def _():
                away.wait_send()

            @pl.when(stays)
            def _():
                near.wait()

        ends.append(finish)

    for p in range(PARTS):
        advance(p, STEPS)
        if p == 1:
            e_advance(STEPS - 1)
        for d in range(2):
            move(
                partial.at[8 * d + z, p], pland.at[hi, j], ps_sem.at[d, p], pr_sem.at[hi, j],
                fin_sem.at[d, p], (y * 4 + p + NSEC - 1) % NSEC, 8 * d + z,
            )
    e_advance(STEPS)
    e_dest = 2 * j + y % 2 + 8 * (y // 2)
    for d in range(2):
        move(
            epart.at[8 * d + z], efin.at[hi], es_sem.at[d], er_sem.at[hi],
            fin_sem.at[d, PARTS], e_dest, 8 * d + z,
        )
    n_copy.wait_recv()
    for h in range(2):
        for n in range(4):
            source = (((s + 1) % NSEC) // 4) * 4 + n

            @pl.when((source != s) | (h != hi))
            def _():
                remote(
                    partial.at[8 * h + z, n], pland.at[h, n], ps_sem.at[h, n], pr_sem.at[h, n],
                    source, 8 * h + z,
                ).wait_recv()

    for end in ends:
        end()
    more = jnp.where(s == NSEC - 1, 0.0, 1.0).astype(F32)
    for n in range(8):
        cols = slice((n // 4) * COLS, (n // 4 + 1) * COLS)
        half = (pland[0, n % 4].astype(F32) + pland[1, n % 4].astype(F32))[:, cols]
        passed_ref[:, n * COLS : (n + 1) * COLS] = (
            (nland[:, n * COLS : (n + 1) * COLS].astype(F32) + half) * more
        ).astype(BF16)

    for n in (2, 3, 4, 5):
        x_copy(n).wait_recv()
    for b in range(2):
        came = dwl[2 + b].astype(F32) + dwl[4 + b].astype(F32)
        for i in range(3):
            cols = slice(i * RANK, (i + 1) * RANK)
            wsum_ref[b, :, cols] = acc[b, skip, cols] + came[i * COLS : (i + 1) * COLS, :]
        last = came[3 * COLS :, :]
        wsum_ref[b, 0:HD, 3 * RANK : COLS] = acc[b, upper, 3 * RANK : COLS] + last[:, 0:64]
        wsum_ref[b, HD:COLS, 3 * RANK : COLS] = acc[b, lower, 3 * RANK : COLS] + last[:, 64:RANK]
    for h in range(2):
        @pl.when((e_dest != s) | (h != hi))
        def _():
            remote(
                epart.at[8 * h + z], efin.at[h], es_sem.at[h], er_sem.at[h], e_dest, 8 * h + z
            ).wait_recv()

    embed_ref[...] = efin[0].astype(F32) + efin[1].astype(F32)
    for copy in sent:
        copy.wait_send()

    @pl.when(j != adder)
    def _():
        down_copy(j).wait_send()
        back_copy(j).wait_send()


def whole_call(ids, q, k, v, g, seg, upt, down, residual, hidden, embedding, weight):
    vm = pl.BlockSpec(memory_space=pltpu.VMEM)
    sm = pl.BlockSpec(memory_space=pltpu.SMEM)
    anys = pl.BlockSpec(memory_space=pl.ANY)
    dma = pltpu.SemaphoreType.DMA
    out = jax.ShapeDtypeStruct
    return pl.pallas_call(
        whole_kernel,
        out_shape=(
            out((COLS, TOKENS), BF16),
            out((COLS, TOKENS), BF16),
            out((COLS, RANK), F32),
            out((COLS, RANK), F32),
            out((2, COLS, COLS), F32),
            out((32, WIDTH), BF16),
            out((32, HD), F32),
        ),
        in_specs=[sm] + [anys] * 4 + [vm] * 3 + [anys] * 4,
        out_specs=(vm,) * 7,
        scratch_shapes=[
            pltpu.VMEM((TOKENS, COLS), BF16),
            pltpu.VMEM((COLS, TOKENS), BF16),
            pltpu.VMEM((4, TOKENS, COLS), BF16),
            pltpu.VMEM((4, 2, TOKENS, WIN), BF16),
            pltpu.VMEM((2, 4 * COLS, COLS), BF16),
            pltpu.VMEM((2, TOKENS, WIN), BF16),
            pltpu.VMEM((TOKENS, WIN), BF16),
            pltpu.VMEM((WIN, RANK), BF16),
            pltpu.VMEM((4, 2 * COLS, RANK), BF16),
            pltpu.VMEM((4, NTP, 32, RANK), BF16),
            pltpu.VMEM((NTP, 32, 2 * RANK), BF16),
            pltpu.VMEM((NTP, 32, 2 * RANK), BF16),
            pltpu.VMEM((32, 2 * RANK), BF16),
            pltpu.VMEM((NTP, 32, 2 * RANK), BF16),
            pltpu.VMEM((4, COLS, TOKENS), BF16),
            pltpu.VMEM((NTP, PARTS, 32, 2 * COLS), BF16),
            pltpu.VMEM((2, PARTS, STEPS, 32, 2 * COLS), BF16),
            pltpu.VMEM((2, 4, 32, 2 * COLS), BF16),
            pltpu.VMEM((32, WIDTH), BF16),
            pltpu.VMEM((4, TOKENS, HD), BF16),
            pltpu.VMEM((4, TOKENS, HD), BF16),
            pltpu.VMEM((NTP, 32, HD), BF16),
            pltpu.VMEM((2, STEPS, 32, HD), BF16),
            pltpu.VMEM((2, 32, HD), BF16),
            pltpu.VMEM((TOKENS, 2 * COLS), F32),
            pltpu.VMEM((2, TOKENS, COLS), BF16),
            pltpu.VMEM((2, WIN, COLS), F32),
            pltpu.VMEM((6, 3 * COLS + HD, RANK), BF16),
            pltpu.VMEM((6, 3 * COLS + HD, RANK), BF16),
            dma((13,)), dma((6,)), dma((6,)), dma((10,)), dma((10,)), dma((3,)), dma((4,)),
            dma((15,)), dma((16,)), dma((15,)), dma((16,)),
            dma((2,)), dma((8,)),
            dma((2, PARTS, STEPS)), dma((2, PARTS, STEPS)),
            dma((6,)), dma((6,)),
            dma((2, 4)), dma((2, 4)), dma((2,)), dma((2,)), dma((2, PARTS + 1)), dma((2,)),
            dma((3,)), dma((4,)), dma((2, STEPS)), dma((2, STEPS)),
        ],
        compiler_params=pltpu.CompilerParams(
            collective_id=0, has_side_effects=True, vmem_limit_bytes=VMEM_LIMIT
        ),
        name="attention_block_backward",
    )(ids, q, k, v, g, seg, upt, down, residual, hidden, embedding, weight)


def copy_kernel(*refs):
    count = (len(refs) - 1) // 3
    sems = refs[-1]
    ins, outs, held = refs[:count], refs[count : 2 * count], refs[2 * count : 3 * count]
    pieces = []
    for n in range(count):
        rows = ins[n].shape[-2]
        if len(ins[n].shape) == 3:
            pieces += [(n, (b, pl.ds(h * HD, HD))) for b in range(2) for h in range(2)]
        elif rows == COLS:
            pieces += [(n, (pl.ds(h * HD, HD),)) for h in range(2)]
        else:
            pieces.append((n, (pl.ds(0, rows),)))

    def copies(a, b, side):
        return [
            pltpu.make_async_copy(a[n].at[at], b[n].at[at], sems.at[side, m])
            for m, (n, at) in enumerate(pieces)
        ]

    coming, going = copies(ins, held, 0), copies(held, outs, 1)
    for copy in coming:
        copy.start()
    for here, on in zip(coming, going):
        here.wait()
        on.start()
    for copy in going:
        copy.wait()


def copy_call(arrays):
    anys = pl.BlockSpec(memory_space=pl.ANY)
    return pl.pallas_call(
        copy_kernel,
        out_shape=tuple(jax.ShapeDtypeStruct(a.shape, a.dtype) for a in arrays),
        in_specs=[anys] * len(arrays),
        out_specs=(anys,) * len(arrays),
        scratch_shapes=[pltpu.VMEM(a.shape, a.dtype) for a in arrays]
        + [pltpu.SemaphoreType.DMA((2, 16))],
        compiler_params=pltpu.CompilerParams(vmem_limit_bytes=VMEM_LIMIT),
        name="hand_over",
    )(*arrays)


def on_device(
    saved_queries,
    saved_keys,
    values,
    attention_output_grad,
    segments,
    hidden,
    embedding,
    section_block_index,
    shared_query_weight,
    adapter_down_factor,
    adapter_up_factor,
    residual,
):
    results = whole_call(
        section_block_index[:, 0],
        saved_queries[0].T,
        saved_keys[0].T,
        values[0].T,
        attention_output_grad[0].T,
        segments[None, :],
        adapter_up_factor[0].T,
        adapter_down_factor[0],
        residual[0],
        hidden[0],
        embedding,
        shared_query_weight,
    )
    kgt, vgt, down_grad, ugt, weight_grad, passed, embed_grad = copy_call(results)
    return (
        kgt.T[None],
        vgt.T[None],
        down_grad[None],
        ugt.T[None],
        weight_grad,
        passed[None],
        embed_grad,
    )


def solution(mesh):
    in_specs = (
        P("section", None, "tp"),
        P("section", None, "tp"),
        P("section", None, "tp"),
        P("section", None, "tp"),
        P(),
        P("section", None, None),
        P(),
        P(),
        P(None, "section", "tp"),
        P("section", "tp", None),
        P("section", None, "tp"),
        P("section", "tp", None),
    )
    out_specs = (
        P("section", None, "tp"),
        P("section", None, "tp"),
        P("section", "tp", None),
        P("section", None, "tp"),
        P(None, "section", "tp"),
        P("section", "tp", None),
        P("tp", "section"),
    )
    return jax.shard_map(
        on_device, mesh=mesh, in_specs=in_specs, out_specs=out_specs, check_vma=False
    )
```
